512 devices in a mesh: ctx: 32 (over y, x, core), ep: 16 (over z).
Axes of the slice: x: 4, y: 4, z: 16, core: 2. Of those that a mesh axis runs over, the one named last changes fastest.
Arguments:
- queries: bfloat16 [64, 64, 576], P('ep'), may hold values from -18 to 18
- latent_cache: bfloat16 [64, 3072, 576], P('ep', 'ctx'), may hold values from -4.5 to 4.5
- lengths: int32 [64], P('ep'), may hold values from 2 to 3072, as said below
- w_uv: bfloat16 [64, 512, 128], P('ctx'), may hold values from -4 to 4
- w_out: bfloat16 [8192, 3584], P('ctx'), may hold values from -0.0625 to 0.0625
- residual: bfloat16 [64, 3584], P('ep', 'ctx'), may hold values from -4 to 4
- norm_gain: float32 [3584], P('ctx'), may hold values from 0.5 to 1.5
- router: bfloat16 [16, 3584], P('ep', 'ctx'), may hold values from -0.09375 to 0.09375
- w_gate: bfloat16 [16, 3584, 2048], P('ep', 'ctx'), may hold values from -0.09375 to 0.09375
- w_up: bfloat16 [16, 3584, 2048], P('ep', 'ctx'), may hold values from -0.09375 to 0.09375
- w_down: bfloat16 [16, 2048, 3584], P('ep', None, 'ctx'), may hold values from -0.125 to 0.125
- expert_ids: int32 [64, 8], P('ep'), may hold values from 0 to 15, all different within a row; in each aligned block of 4 rows (0 to 3, 4 to 7, ...) at most 4 rows name the same one
Outputs:
- mixed: float32 [64, 3584], P('ep', 'ctx')
The draws below stay inside these ranges and needn't reach their ends.
Inputs may be any that keep to these rules, and one draw needn't show every extreme that they name: `expert_ids`: each row names 8 different experts; the 4 rows of one ep index name one expert at most 4 times, and exactly 4 times for some expert. `lengths`: every row reads at least its first two positions; some row reads all 3072.
All inputs are finite; a program needn't handle non-finite values.
Results may differ from the reference program's by a relative error of at most 0.019.
Values may be sent and summed in bfloat16 or wider, within the bound.
A program may use at most 64 MiB of HBM per device.

```python
import math
import jax
import jax.numpy as jnp
import numpy as np
from jax import lax

D = 3584
HEADS = 64
LATENT = 512
ROPE = 64
VDIM = 128
FF = 2048
ROWS_DEV = 4
ROWS = 64
CTX = 3072
EXPERTS = 16
TOP = 8
CAP = 4


def draw_latent_cache(key, part):
    key = jax.random.fold_in(key, 7)
    return jnp.clip(jax.random.normal(key, (ROWS, CTX, LATENT + ROPE), jnp.float32), -4.0, 4.0).astype(jnp.bfloat16)


def draw_queries(key, part):
    key = jax.random.fold_in(key, 8)
    return jnp.clip(jax.random.normal(key, (ROWS, HEADS, LATENT + ROPE), jnp.float32), -4.0, 4.0).astype(jnp.bfloat16)


def draw_lengths(key, part):
    key = jax.random.fold_in(key, 9)
    drawn = jax.random.randint(key, (ROWS,), 2, CTX + 1)
    picked = jax.random.randint(jax.random.fold_in(key, 1), (), 0, ROWS)
    return jnp.where(jnp.arange(ROWS) == picked, CTX, drawn).astype(jnp.int32)


def block_scale(key, shape, shards, least, largest):
    gain, own = 1.0, jax.random.fold_in(key, 6)
    for dim, blocks in shards:
        draws = jnp.exp(jax.random.uniform(jax.random.fold_in(own, dim), (blocks,), jnp.float32, least / len(shards), largest / len(shards)))
        gain = gain * jnp.repeat(draws, shape[dim] // blocks).reshape([-1 if axis == dim else 1 for axis in range(len(shape))])
    return gain


def deal_out(stream_key, own, number, rows, amount, top, bound, slope):
    ranking = jax.random.permutation(stream_key, amount)
    crowded, usual = shares(amount, rows * top, bound, slope, True), shares(amount, rows * top, bound, slope, False)
    places = jnp.arange(amount)

    def named(tallies, turn):
        used = int((tallies > 0).sum())
        fixed = max(1, used // 4)
        moved = fixed + (places - fixed + turn * (used - fixed)) % max(1, amount - fixed)
        return jnp.zeros((amount,), jnp.int32).at[ranking[jnp.where(places < fixed, places, moved)]].set(jnp.asarray(tallies, jnp.int32))

    tallies = jnp.where(number % 4 == 0, named(crowded, number // 4), named(usual, number - number // 4 - 1))
    mixed = jax.random.permutation(jax.random.fold_in(own, 3), amount)
    source_of, taker = mixed[0:amount // 2 * 2:2], mixed[1:amount // 2 * 2:2]
    slack = jnp.minimum(tallies[source_of] - 1, bound - tallies[taker]) // 2
    slack = jnp.where((source_of == ranking[0]) | (taker == ranking[0]) | (tallies[taker] == 0), 0, jnp.maximum(slack, 0))
    moved = jax.random.randint(jax.random.fold_in(own, 4), (amount // 2,), 0, 1 << 20) % (slack + 1)
    tallies = tallies.at[source_of].add(-moved).at[taker].add(moved)
    labels = jnp.searchsorted(jnp.cumsum(tallies), jnp.arange(rows * top), side="right").astype(jnp.int32)
    listing = labels.reshape(top, rows).T
    listing = listing[jax.random.permutation(jax.random.fold_in(own, 1), rows)]
    turn = jax.random.randint(jax.random.fold_in(own, 2), (rows, 1), 0, top)
    return jnp.take_along_axis(listing, (jnp.arange(top)[None, :] + turn) % top, axis=1)


def shares(count, total, reach, slope, full):
    loads = [(1 << 20) // math.isqrt(grade ** slope) + 1 for grade in range(1, count + 1)]
    largest = reach if full else min(reach, max(-(-total // count), total * loads[0] // sum(loads)))
    least = 1 if total - largest >= count - 1 else 0
    given, surplus = [largest] + [least] * (count - 1), total - largest - least * (count - 1)
    while surplus > 0:
        free = [i for i in range(1, count) if given[i] < largest] or [i for i in range(1, count) if given[i] < reach]
        pool, budget = sum([loads[i] for i in free]), surplus
        for i in free:
            addition = min(reach - given[i], max(1, budget * loads[i] // pool), surplus)
            given[i] = given[i] + addition
            surplus = surplus - addition
    return np.array(given)


def bell_draw(stream_key, shape, deviation, bound, cuts=(), kind=jnp.bfloat16):
    level = block_scale(stream_key, shape, cuts, -0.22, 0.18) if cuts else 1.0
    result = jax.random.normal(stream_key, shape, jnp.float32) * deviation * level
    return jnp.minimum(jnp.maximum(result, -bound), bound).astype(kind)


def setup_inputs(seed: int = 0) -> dict:
    key_list = jax.random.split(jax.random.key(seed), 13)
    queries = draw_queries(jax.random.fold_in(key_list[12], 71), 0)
    latent_cache = draw_latent_cache(jax.random.fold_in(key_list[12], 71), 0)
    lengths = draw_lengths(jax.random.fold_in(key_list[12], 71), 0)
    w_uv = bell_draw(key_list[3], (HEADS, LATENT, VDIM), 0.3, 4.0, ((0, 32),))
    w_out = bell_draw(key_list[4], (HEADS * VDIM, D), (HEADS * VDIM) ** -0.5, 0.0625, ((0, 32),))
    residual = bell_draw(key_list[5], (ROWS, D), 0.5, 4.0, ((0, 16), (1, 32)))
    norm_gain = jnp.clip(1.0 + 0.1 * jax.random.normal(key_list[6], (D,), jnp.float32), 0.5, 1.5)
    router = bell_draw(key_list[7], (EXPERTS, D), D ** -0.5, 0.09375, ((0, 16), (1, 32)))
    w_gate = bell_draw(key_list[8], (EXPERTS, D, FF), D ** -0.5, 0.09375, ((0, 16), (1, 32)))
    w_up = bell_draw(key_list[9], (EXPERTS, D, FF), D ** -0.5, 0.09375, ((0, 16), (1, 32)))
    w_down = bell_draw(key_list[10], (EXPERTS, FF, D), FF ** -0.5, 0.125, ((0, 16), (2, 32)))
    expert_ids_keys = jax.random.split(jax.random.fold_in(key_list[11], 1), ROWS // ROWS_DEV)
    expert_ids_turns = jax.random.permutation(jax.random.fold_in(key_list[11], 3), ROWS // ROWS_DEV)
    expert_ids = jax.vmap(lambda own, number: deal_out(jax.random.fold_in(key_list[11], 2), own, number, ROWS_DEV, EXPERTS, TOP, CAP, 2))(expert_ids_keys, expert_ids_turns).reshape((ROWS, TOP))
    return dict(queries=queries, latent_cache=latent_cache, lengths=lengths, w_uv=w_uv, w_out=w_out, residual=residual, norm_gain=norm_gain, router=router, w_gate=w_gate, w_up=w_up, w_down=w_down, expert_ids=expert_ids)


score_scale = 192.0 ** (-0.5)
floor_value = -1e+30
norm_eps = 1e-06
route_scale = 2.5

def reference(queries, latent_cache, lengths, w_uv, w_out, residual, norm_gain, router, w_gate, w_up, w_down, expert_ids):

    def one_row(packed):
        query_rows, cache_rows, length = packed
        scores = jnp.dot(query_rows, cache_rows.T, preferred_element_type=jnp.float32) * score_scale
        valid = (jnp.arange(CTX) < length)[None, :]
        masked = jnp.where(valid, scores, floor_value)
        peak = lax.optimization_barrier(jnp.max(masked, axis=1))
        weights = jnp.where(valid, jnp.exp(masked - peak[:, None]), 0.0).astype(jnp.bfloat16)
        totals = lax.optimization_barrier(jnp.sum(weights.astype(jnp.float32), axis=1))
        summed = jnp.dot(weights, cache_rows[:, :LATENT], preferred_element_type=jnp.float32)
        return (summed / totals[:, None]).astype(jnp.bfloat16)
    latent_out = lax.map(one_row, (queries, latent_cache, lengths))
    value_rows = jnp.einsum('rhl,hlv->rhv', latent_out.astype(jnp.float32), w_uv.astype(jnp.float32))
    value_rows = value_rows.astype(jnp.bfloat16).reshape(ROWS, HEADS * VDIM)
    stream = residual.astype(jnp.float32) + jnp.dot(value_rows, w_out, preferred_element_type=jnp.float32)
    hidden = stream.astype(jnp.bfloat16)
    wide = hidden.astype(jnp.float32)
    inverse = lax.rsqrt(lax.optimization_barrier(jnp.mean(wide * wide, axis=1)) + norm_eps)
    scaled = (wide * norm_gain).astype(jnp.bfloat16)

    def expert_step(carry, index):
        numer, denom = carry
        gate = jnp.dot(scaled, w_gate[index], preferred_element_type=jnp.float32) * inverse[:, None]
        up_value = jnp.dot(scaled, w_up[index], preferred_element_type=jnp.float32) * inverse[:, None]
        logit = jnp.dot(scaled, router[index], preferred_element_type=jnp.float32) * inverse
        score = lax.optimization_barrier(jax.nn.sigmoid(logit).astype(jnp.bfloat16)).astype(jnp.float32)
        act = (jax.nn.silu(gate) * up_value).astype(jnp.bfloat16)
        produced = jnp.dot(act, w_down[index], preferred_element_type=jnp.float32)
        contribution = lax.optimization_barrier((produced * score[:, None]).astype(jnp.bfloat16)).astype(jnp.float32)
        chosen = lax.optimization_barrier(jnp.sum((expert_ids == index).astype(jnp.float32), axis=1))
        return ((numer + chosen[:, None] * contribution, denom + chosen * score), None)
    start = (jnp.zeros((ROWS, D), jnp.float32), jnp.zeros((ROWS,), jnp.float32))
    (numer, denom), unused = lax.scan(expert_step, start, jnp.arange(EXPERTS, dtype=jnp.int32))
    mixed = stream + route_scale * numer / denom[:, None]
    return mixed
```

```python
import functools

import jax
import jax.numpy as jnp
from jax import lax
from jax.experimental import pallas as pl
from jax.experimental.pallas import tpu as pltpu
from jax.sharding import PartitionSpec as P

SCALE = 192.0 ** (-0.5)
FLOOR = -1e30
EPS = 1e-06
ROUTE = 2.5
LATENT = 512
WIDE = 128
MESH = pl.DeviceIdType.MESH
BF16, F32, I32 = jnp.bfloat16, jnp.float32, jnp.int32


def iota(shape, dim):
    return lax.broadcasted_iota(I32, shape, dim)


def split_two(x):
    high = x.astype(BF16).astype(F32)
    return high, x - high


def kernel(
    nc,
    ne,
    q_h, cache_h, len_h, wuv_h, wout_h, res_h, gain_h, router_h, wg_h, wu_h, wd_h, ids_h,
    out_ref,
    q_v, cache_v, len_s, wuv_v, wout_v, res_v, gain_v, router_v, wg_v, wu_v, wd_v, ids_v,
    pack, hit_v, st_v, hid_v,
    s1, r1, s2, r2, r3, s4, r4, s5, r5, s6, r6,
    load_sem, pair_send, pair_recv, ssem, rsem,
):
    nk, half = nc // 2, ne // 2
    width = res_h.shape[1]
    span = cache_h.shape[1]
    rows = 8 * nc
    batch = 4 * half
    c, e = lax.axis_index("ctx"), lax.axis_index("ep")
    k, core = c // 2, lax.rem(c, 2)
    side = e // half
    owner = core == side
    partner = 2 * k + 1 - core

    def load(n, src, dst):
        return pltpu.make_async_copy(src, dst, load_sem.at[n])

    loads = [
        load(0, q_h, q_v),
        load(1, cache_h, cache_v),
        load(2, len_h, len_s),
        load(3, res_h, res_v),
        load(4, gain_h, gain_v),
        load(5, router_h, router_v),
        load(6, ids_h, ids_v),
        load(7, wuv_h, wuv_v),
        load(8, wout_h, wout_v),
        load(9, wg_h.at[0], wg_v.at[core, pl.ds(0, width)]),
        load(10, wu_h.at[0], wu_v.at[core, pl.ds(0, width)]),
        load(11, wd_h.at[0], wd_v.at[core]),
    ]
    for one in loads:
        one.start()

    barrier = pltpu.get_barrier_semaphore()

    def greet_ctx(i, _):
        pl.semaphore_signal(barrier, inc=1, device_id=(lax.rem(c + i, nc), e), device_id_type=MESH)
        return 0

    def greet_ep(i, _):
        for f in range(2):
            pl.semaphore_signal(
                barrier, inc=1, device_id=(2 * k + f, lax.rem(e + i, ne)), device_id_type=MESH
            )
        return 0

    lax.fori_loop(1, nc, greet_ctx, 0)
    lax.fori_loop(1, ne, greet_ep, 0)

    def remote(src, dst, send, recv, to):
        return pltpu.make_async_remote_copy(
            src_ref=src, dst_ref=dst, send_sem=send, recv_sem=recv, device_id=to, device_id_type=MESH
        )

    def drain(ref, sem):
        pltpu.make_async_copy(ref, ref, sem).wait()

    for one in loads[2:7]:
        one.wait()
    pack[pl.ds(core, 1)] = jnp.zeros((1, 16, WIDE), F32)
    wide_res = res_v[...].astype(F32)
    pack[core, 0:8, 0:width] = jnp.concatenate([wide_res, wide_res], axis=0)
    pack[core, 8:9, 0:width] = gain_v[...]
    pack[core, 9:10, 0:width] = router_v[...].astype(F32)
    blank = jnp.zeros((2, WIDE - width, wg_v.shape[2]), BF16)
    wg_v[:, width:WIDE, :] = blank
    wu_v[:, width:WIDE, :] = blank
    ids8 = jnp.concatenate([ids_v[...], ids_v[...]], axis=0)
    for x in range(ne):
        hit = jnp.max(jnp.where(ids8 == x, 1.0, 0.0), axis=1, keepdims=True)
        hit_v[x] = jnp.broadcast_to(hit, (8, WIDE))

    loads[0].wait()
    row = iota((rows, rows), 0)
    want = (row & 3) * (2 * nc) + 2 * (row >> 3) + ((row >> 2) & 1)
    order = jnp.where(iota((rows, rows), 1) == want, 1.0, 0.0).astype(BF16)
    q = q_v[...].reshape(rows, q_v.shape[2])
    q = jnp.dot(order, q, preferred_element_type=F32).astype(BF16)
    loads[1].wait()
    keys = cache_v[...].reshape(4 * span, cache_v.shape[2])
    scores = lax.dot_general(q, keys, (((1,), (1,)), ((), ())), preferred_element_type=F32) * SCALE
    col = iota((1, 4 * span), 1)
    col_row = jnp.zeros_like(col)
    limit = jnp.full_like(col, len_s[0])
    for r in range(1, 4):
        past = col >= r * span
        col_row = jnp.where(past, r, col_row)
        limit = jnp.where(past, len_s[r], limit)
    position = c * span + col - col_row * span
    col_row = jnp.where(position < limit, col_row, -1)
    valid = (iota((rows, 4 * span), 0) & 3) == col_row
    masked = jnp.where(valid, scores, FLOOR)
    peak = jnp.max(masked, axis=1, keepdims=True).astype(BF16).astype(F32)
    weights = jnp.where(valid, jnp.exp(masked - peak), 0.0).astype(BF16)
    total = jnp.sum(weights.astype(F32), axis=1, keepdims=True)
    summed = jnp.dot(weights, keys[:, :LATENT], preferred_element_type=F32)
    summed = summed.reshape(nc, 8, LATENT)
    hl = LATENT // 2
    s1[:, :, 0:hl] = jnp.concatenate([summed[:, :, 0:hl], summed[:, :, hl:]], axis=1).astype(BF16)
    high, low = split_two(total)
    peaks = jnp.broadcast_to(peak, (rows, WIDE)).reshape(nc, 8, WIDE)
    totals = jnp.where(iota((rows, WIDE), 1) < 64, high, low).reshape(nc, 8, WIDE)
    s1[:, :, hl:] = jnp.concatenate([peaks, totals], axis=1).astype(BF16)
    r1[pl.ds(c, 1)] = s1[pl.ds(c, 1)]

    pl.semaphore_wait(barrier, nc - 1 + 2 * (ne - 1))

    def send_1(i, _):
        d = lax.rem(c + i, nc)
        remote(s1.at[d], r1.at[c], ssem.at[0], rsem.at[0], (d, e)).start()
        return 0

    lax.fori_loop(1, nc, send_1, 0)

    mine = pl.ds(0, width)
    swaps = [
        remote(pack.at[core], pack.at[core], pair_send.at[0], pair_recv.at[0], (partner, e)),
        remote(wg_h.at[0], wg_v.at[core, mine], pair_send.at[1], pair_recv.at[1], (partner, e)),
        remote(wu_h.at[0], wu_v.at[core, mine], pair_send.at[2], pair_recv.at[2], (partner, e)),
        remote(wd_h.at[0], wd_v.at[core], pair_send.at[3], pair_recv.at[3], (partner, e)),
    ]
    for one in swaps:
        one.start()

    drain(r1.at[pl.ds(0, nc - 1)], rsem.at[0])
    stats = r1[:, :, hl:].astype(F32)
    peaks = stats[:, 0:8]
    factor = jnp.exp(peaks - jnp.max(peaks, axis=0)[None])
    denom = jnp.sum(factor * stats[:, 8:16], axis=0)
    denom = denom[:, 0:1] + denom[:, 64:65]
    columns = []
    for top in range(2):
        for a in range(0, hl, WIDE):
            block = r1[:, :, a : a + WIDE].astype(F32)[:, 8 * top : 8 * top + 8]
            columns.append(jnp.sum(factor * block, axis=0))
    latent = (jnp.concatenate(columns, axis=1) / denom).astype(BF16)

    loads[7].wait()
    first = jnp.dot(latent, wuv_v[0], preferred_element_type=F32)
    second = jnp.dot(latent, wuv_v[1], preferred_element_type=F32)
    upper = iota((8, WIDE), 0) < 4
    lane = iota((8, WIDE), 1)
    values = jnp.concatenate(
        [
            jnp.where(upper, first, pltpu.roll(first, 4, 0)),
            jnp.where(upper, pltpu.roll(second, 4, 0), second),
        ],
        axis=1,
    ).astype(BF16)
    loads[8].wait()
    group = min(4, nk)
    for g in range(0, nk, group):
        begin, size = 2 * width * g, 2 * width * group
        part = jnp.dot(values, wout_v[:, begin : begin + size], preferred_element_type=F32)
        part = jnp.concatenate([part, jnp.zeros((8, WIDE), F32)], axis=1)
        for i in range(group):
            a = 2 * width * i
            s2[g + i] = jnp.where(upper, part[:, a : a + WIDE], part[:, a + width : a + width + WIDE])

    def send_2(i, _):
        d = lax.rem(k + i, nk)
        remote(s2.at[d], r2.at[c], ssem.at[1], rsem.at[1], (2 * d + side, e)).start()
        return 0

    @pl.when(owner)
    def _():
        r2[pl.ds(c, 1)] = s2[pl.ds(k, 1)]

    @pl.when(jnp.logical_not(owner))
    def _():
        send_2(0, 0)

    lax.fori_loop(1, nk, send_2, 0)

    swaps[0].wait_recv()

    @pl.when(owner)
    def _():
        drain(r2.at[pl.ds(0, nc - 1)], rsem.at[1])
        stream = jnp.sum(r2[...], axis=0) + jnp.where(upper, pack[0, 0:8], pack[1, 0:8])
        stream = jnp.where(lane < width, stream, 0.0)
        hidden = stream.astype(BF16).astype(F32)
        hid_v[...] = hidden
        st_v[...] = stream
        r3[pl.ds(lax.rem(e, half), 1)] = hidden[None]

        def send_3(i, _):
            z = lax.rem(e + i, ne)
            remote(hid_v, r3.at[lax.rem(e, half)], ssem.at[2], rsem.at[2], (c, z)).start()
            return 0

        lax.fori_loop(1, ne, send_3, 0)
        remote(st_v, st_v, pair_send.at[4], pair_recv.at[4], (partner, e)).start()
        drain(r3.at[pl.ds(0, half - 1)], rsem.at[2])

    @pl.when(jnp.logical_not(owner))
    def _():
        drain(r3, rsem.at[2])

    got = r3[...]
    turned = pltpu.roll(got, 4, 1)
    top3 = iota((half // 2, 8, WIDE), 1) < 4
    got, turned = got.reshape(half // 2, 2, 8, WIDE), turned.reshape(half // 2, 2, 8, WIDE)
    tokens = [
        jnp.where(top3, got[:, 0], turned[:, 1]).reshape(batch, WIDE),
        jnp.where(top3, turned[:, 0], got[:, 1]).reshape(batch, WIDE),
    ]
    squares = jnp.sum(tokens[0] * tokens[0] + tokens[1] * tokens[1], axis=1, keepdims=True)
    scaled = [(tokens[f] * pack[f, 8:9, :]).astype(BF16) for f in range(2)]
    logits = jnp.sum(
        scaled[0].astype(F32) * pack[0, 9:10, :] + scaled[1].astype(F32) * pack[1, 9:10, :],
        axis=1,
        keepdims=True,
    )
    scaled = jnp.concatenate(scaled, axis=1)

    lane16 = iota((16, WIDE), 1)
    block = jnp.zeros((16, WIDE), F32)
    place = 0
    for stat in (squares, logits):
        for piece in split_two(stat):
            for a in range(0, batch, 16):
                block = jnp.where(lane16 == place, piece[a : a + 16], block)
                place += 1
    block = block.astype(BF16)
    for n in (9, 10):
        loads[n].wait()
        swaps[n - 8].wait_recv()
    gate = jnp.dot(scaled, wg_v[...].reshape(2 * WIDE, -1), preferred_element_type=F32).astype(BF16)
    up = jnp.dot(scaled, wu_v[...].reshape(2 * WIDE, -1), preferred_element_type=F32).astype(BF16)
    for d in range(nk):
        s4[d, 0:batch] = gate[:, d * WIDE : (d + 1) * WIDE]
        s4[d, batch : 2 * batch] = up[:, d * WIDE : (d + 1) * WIDE]
        s4[d, 2 * batch :] = block
    r4[pl.ds(k, 1)] = s4[pl.ds(k, 1)]

    def send_4(i, _):
        d = lax.rem(k + i, nk)
        remote(s4.at[d], r4.at[k], ssem.at[3], rsem.at[3], (2 * d + core, e)).start()
        return 0

    lax.fori_loop(1, nk, send_4, 0)
    drain(r4.at[pl.ds(0, nk - 1)], rsem.at[3])
    sums = jnp.sum(r4[...].astype(F32), axis=0)
    gate, up, block = sums[0:batch], sums[batch : 2 * batch], sums[2 * batch :]
    parts = batch // 16

    def column(n):
        pair = block[:, n * parts : (n + 1) * parts] + block[:, (n + 1) * parts : (n + 2) * parts]
        return jnp.concatenate([pair[:, a : a + 1] for a in range(parts)], axis=0)

    inverse = lax.rsqrt(column(0) / (width * nc) + EPS)
    score = jax.nn.sigmoid(column(2) * inverse).astype(BF16).astype(F32)
    gate = gate * inverse
    act = gate / (1.0 + jnp.exp(-gate)) * (up * inverse) * score
    act = act.astype(BF16)

    s5[...] = act
    r5[pl.ds(k, 1)] = act[None]

    def send_5(i, _):
        d = lax.rem(k + i, nk)
        remote(s5, r5.at[k], ssem.at[4], rsem.at[4], (2 * d + core, e)).start()
        return 0

    lax.fori_loop(1, nk, send_5, 0)
    loads[11].wait()
    swaps[3].wait_recv()
    drain(r5.at[pl.ds(0, nk - 1)], rsem.at[4])
    act = jnp.concatenate([r5[d] for d in range(nk)], axis=1)
    shown = jnp.broadcast_to(score, (batch, WIDE - width))
    for f in range(2):
        made = jnp.dot(act, wd_v[f], preferred_element_type=F32)
        made = jnp.concatenate([made, shown], axis=1)
        s6[f] = made.reshape(half // 2, 8, WIDE)

    def send_6(i, _):
        t = lax.rem(e + i, half)
        z = half * core + t
        for f in range(2):
            @pl.when(jnp.logical_not((f == core) & (z == e)))
            def _():
                remote(s6.at[f, t // 2], r6.at[e], ssem.at[5], rsem.at[5], (2 * k + f, z)).start()
        return 0

    lax.fori_loop(0, half, send_6, 0)

    @pl.when(owner)
    def _():
        r6[pl.ds(e, 1)] = s6[core, pl.ds(lax.rem(e, half) // 2, 1)]
        drain(r6.at[pl.ds(0, ne - 1)], rsem.at[5])

    @pl.when(jnp.logical_not(owner))
    def _():
        drain(r6, rsem.at[5])
        pltpu.make_async_copy(st_v, st_v, pair_recv.at[4]).wait()

    mixed = jnp.sum(jnp.where(hit_v[...] > 0.0, r6[...], 0.0), axis=0)
    mixed = jnp.where(lax.rem(e, 2) == 1, pltpu.roll(mixed, 4, 0), mixed)[0:4]
    stream = st_v[...]
    stream = jnp.where(core == 1, pltpu.roll(stream, 4, 0), stream)[0:4]
    out_ref[...] = stream[:, 0:width] + ROUTE * mixed[:, 0:width] / mixed[:, width : width + 1]

    drain(s1.at[pl.ds(0, nc - 1)], ssem.at[0])
    drain(s2.at[pl.ds(0, nk - 1)], ssem.at[1])
    drain(s4.at[pl.ds(0, nk - 1)], ssem.at[3])
    drain(r5.at[pl.ds(0, nk - 1)], ssem.at[4])
    drain(r6.at[pl.ds(0, ne - 1)], ssem.at[5])

    @pl.when(owner)
    def _():
        drain(r6.at[pl.ds(0, ne - 1)], ssem.at[2])
        pltpu.make_async_copy(st_v, st_v, pair_send.at[4]).wait()

    @pl.when(jnp.logical_not(owner))
    def _():
        drain(s2.at[0], ssem.at[1])
        drain(r6.at[0], ssem.at[5])

    for one in swaps:
        one.wait_send()


def per_device(nc, ne, *args):
    (queries, cache, lengths, w_uv, w_out, residual, gain, router, w_gate, w_up, w_down, ids) = args
    nk, half = nc // 2, ne // 2
    width, ff = w_gate.shape[1], w_gate.shape[2]
    batch = 4 * half
    any_space = pl.BlockSpec(memory_space=pl.ANY)
    vmem = lambda *shape, dtype=F32: pltpu.VMEM(shape, dtype)
    half_type = functools.partial(vmem, dtype=BF16)
    like = lambda x: pltpu.VMEM(x.shape, x.dtype)
    gain = gain.reshape(1, width)
    scratch = [
        like(queries), like(cache), pltpu.SMEM(lengths.shape, I32), like(w_uv), like(w_out), like(residual),
        like(gain), like(router),
        half_type(2, WIDE, ff), half_type(2, WIDE, ff), half_type(2, ff, width), like(ids),
        vmem(2, 16, WIDE), vmem(ne, 8, WIDE), vmem(8, WIDE), vmem(8, WIDE),
        half_type(nc, 16, LATENT // 2 + WIDE), half_type(nc, 16, LATENT // 2 + WIDE),
        vmem(nk, 8, WIDE), vmem(nc, 8, WIDE),
        vmem(half, 8, WIDE),
        half_type(nk, 2 * batch + 16, WIDE), half_type(nk, 2 * batch + 16, WIDE),
        half_type(batch, WIDE), half_type(nk, batch, WIDE),
        vmem(2, half // 2, 8, WIDE), vmem(ne, 8, WIDE),
        pltpu.SemaphoreType.DMA((12,)),
        pltpu.SemaphoreType.DMA((5,)), pltpu.SemaphoreType.DMA((5,)),
        pltpu.SemaphoreType.DMA((6,)), pltpu.SemaphoreType.DMA((6,)),
    ]
    return pl.pallas_call(
        functools.partial(kernel, nc, ne),
        out_shape=jax.ShapeDtypeStruct((4, width), F32),
        in_specs=[any_space] * 12,
        out_specs=pl.BlockSpec(memory_space=pltpu.VMEM),
        scratch_shapes=scratch,
        compiler_params=pltpu.CompilerParams(
            collective_id=0, has_side_effects=True, vmem_limit_bytes=40 * 1024 * 1024
        ),
    )(queries, cache, lengths, w_uv, w_out, residual, gain, router, w_gate, w_up, w_down, ids)


def solution(mesh):
    in_specs = (
        P("ep", None, None),
        P("ep", "ctx", None),
        P("ep"),
        P("ctx", None, None),
        P("ctx", None),
        P("ep", "ctx"),
        P("ctx"),
        P("ep", "ctx"),
        P("ep", "ctx", None),
        P("ep", "ctx", None),
        P("ep", None, "ctx"),
        P("ep", None),
    )
    return jax.shard_map(
        functools.partial(per_device, mesh.shape["ctx"], mesh.shape["ep"]),
        mesh=mesh, in_specs=in_specs, out_specs=P("ep", "ctx"), check_vma=False,
    )
```

```python
import functools

import jax
import jax.numpy as jnp
from jax import lax
from jax.experimental import pallas as pl
from jax.experimental.pallas import tpu as pltpu
from jax.sharding import PartitionSpec as P

SCALE = 192.0 ** (-0.5)
FLOOR = -1e30
EPS = 1e-06
ROUTE = 2.5
LATENT = 512
WIDE = 128
MESH = pl.DeviceIdType.MESH
BF16, F32, I32 = jnp.bfloat16, jnp.float32, jnp.int32


def iota(shape, dim):
    return lax.broadcasted_iota(I32, shape, dim)


def split_two(x):
    high = x.astype(BF16).astype(F32)
    return high, x - high


def kernel(
    nc,
    ne,
    q_h, cache_h, len_h, wuv_h, wout_h, res_h, gain_h, router_h, wg_h, wu_h, wd_h, ids_h,
    out_ref,
    q_v, cache_v, len_s, wuv_v, wout_v, res_v, gain_v, router_v, wg_v, wu_v, wd_v, ids_v,
    pack, hit_v, st_v, hid_v,
    s1, r1, s2, r2, r3, s4, r4, s5, r5, s6, r6,
    load_sem, pair_send, pair_recv, ssem, rsem, hello,
):
    nk, half = nc // 2, ne // 2
    width = res_h.shape[1]
    span = cache_h.shape[1]
    rows = 8 * nc
    batch = 4 * half
    c, e = lax.axis_index("ctx"), lax.axis_index("ep")
    k, core = c // 2, lax.rem(c, 2)
    side = e // half
    owner = core == side
    partner = 2 * k + 1 - core

    def load(n, src, dst):
        return pltpu.make_async_copy(src, dst, load_sem.at[n])

    loads = [
        load(0, q_h, q_v),
        load(1, cache_h, cache_v),
        load(2, len_h, len_s),
        load(3, res_h, res_v),
        load(4, gain_h, gain_v),
        load(5, router_h, router_v),
        load(6, ids_h, ids_v),
        load(7, wuv_h, wuv_v),
        load(8, wout_h, wout_v),
        load(9, wg_h.at[0], wg_v.at[core, pl.ds(0, width)]),
        load(10, wu_h.at[0], wu_v.at[core, pl.ds(0, width)]),
        load(11, wd_h.at[0], wd_v.at[core, pl.ds(0, width)]),
    ]
    for one in loads:
        one.start()

    place = jnp.where((core == 1) & (e >= half), ne - 1 - (e - half), e)
    base = core * half
    source = (place >= base) & (place < base + half)

    def at_place(p):
        return (c, jnp.where((core == 1) & (p >= half), ne - 1 - (p - half), p))

    barrier = pltpu.get_barrier_semaphore()

    def greet(to):
        pl.semaphore_signal(barrier, inc=1, device_id=to, device_id_type=MESH)

    def greet_ctx(i, _):
        greet((lax.rem(c + i, nc), e))
        return 0

    def greet_ep(p, _):
        greet(at_place(p))
        return 0

    lax.fori_loop(1, nc, greet_ctx, 0)
    first_up = jnp.where(core == 0, jnp.where(source, place + 1, ne), jnp.maximum(place + 1, half))
    lax.fori_loop(first_up, ne, greet_ep, 0)
    greeted = jnp.where(core == 0, jnp.minimum(place, half), jnp.where(source, place, 0))

    def answer(p, _):
        pl.semaphore_signal(hello, inc=1, device_id=at_place(p), device_id_type=MESH)
        return 0

    xs = 4 if nk % 4 == 0 else nk
    ys = nk // xs
    chips = [(dy, dx) for dy in range(ys) for dx in range(xs) if (dy, dx) != (0, 0)]
    chips.sort(key=lambda o: -min(o[0], ys - o[0]) - min(o[1], xs - o[1]))

    def chip_at(offset):
        return lax.rem(k // xs + offset[0], ys) * xs + lax.rem(k + offset[1], xs)

    far = sorted(range(1, ne), key=lambda i: -min(i, ne - i))

    def remote(src, dst, send, recv, to):
        return pltpu.make_async_remote_copy(
            src_ref=src, dst_ref=dst, send_sem=send, recv_sem=recv, device_id=to, device_id_type=MESH
        )

    def drain(ref, sem):
        pltpu.make_async_copy(ref, ref, sem).wait()

    for one in loads[2:7]:
        one.wait()
    pack[pl.ds(core, 1)] = jnp.zeros((1, 16, WIDE), F32)
    wide_res = res_v[...].astype(F32)
    pack[core, 0:8, 0:width] = jnp.concatenate([wide_res, wide_res], axis=0)
    pack[core, 8:9, 0:width] = gain_v[...]
    pack[core, 9:10, 0:width] = router_v[...].astype(F32)
    blank = jnp.zeros((2, WIDE - width, wg_v.shape[2]), BF16)
    wg_v[:, width:WIDE, :] = blank
    wu_v[:, width:WIDE, :] = blank
    wd_v[:, width:WIDE, :] = blank
    ids = ids_v[...]
    for x in range(ne):
        hit = jnp.max(jnp.where(ids == x, 1.0, 0.0), axis=1, keepdims=True)
        hit_v[x] = jnp.broadcast_to(hit, (4, WIDE))

    loads[0].wait()
    row = iota((rows, rows), 0)
    want = (row & 3) * (2 * nc) + 2 * (row >> 3) + ((row >> 2) & 1)
    order = jnp.where(iota((rows, rows), 1) == want, 1.0, 0.0).astype(BF16)
    q = q_v[...].reshape(rows, q_v.shape[2])
    q = jnp.dot(order, q, preferred_element_type=F32).astype(BF16)
    loads[1].wait()
    keys = cache_v[...].reshape(4 * span, cache_v.shape[2])
    scores = lax.dot_general(q, keys, (((1,), (1,)), ((), ())), preferred_element_type=F32) * SCALE
    col = iota((1, 4 * span), 1)
    col_row = jnp.zeros_like(col)
    limit = jnp.full_like(col, len_s[0])
    for r in range(1, 4):
        past = col >= r * span
        col_row = jnp.where(past, r, col_row)
        limit = jnp.where(past, len_s[r], limit)
    position = c * span + col - col_row * span
    col_row = jnp.where(position < limit, col_row, -1)
    valid = (iota((rows, 4 * span), 0) & 3) == col_row
    masked = jnp.where(valid, scores, FLOOR)
    peak = jnp.max(masked, axis=1, keepdims=True).astype(BF16).astype(F32)
    weights = jnp.where(valid, jnp.exp(masked - peak), 0.0).astype(BF16)
    total = jnp.sum(weights.astype(F32), axis=1, keepdims=True)
    summed = jnp.dot(weights, keys[:, :LATENT], preferred_element_type=F32)
    summed = summed.reshape(nc, 8, LATENT)
    hl = LATENT // 2
    s1[:, :, 0:hl] = jnp.concatenate([summed[:, :, 0:hl], summed[:, :, hl:]], axis=1).astype(BF16)
    high, low = split_two(total)
    peaks = jnp.broadcast_to(peak, (rows, WIDE)).reshape(nc, 8, WIDE)
    totals = jnp.where(iota((rows, WIDE), 1) < 64, high, low).reshape(nc, 8, WIDE)
    s1[:, :, hl:] = jnp.concatenate([peaks, totals], axis=1).astype(BF16)
    r1[pl.ds(c, 1)] = s1[pl.ds(c, 1)]

    pl.semaphore_wait(barrier, nc - 1 + greeted)
    lax.fori_loop(base, jnp.where(source | (core == 0), jnp.minimum(place, base + half), base), answer, 0)

    def send_1(d):
        remote(s1.at[d], r1.at[c], ssem.at[0], rsem.at[0], (d, e)).start()

    for offset in chips:
        for f in range(2):
            send_1(2 * chip_at(offset) + f)
    send_1(partner)

    mine = pl.ds(0, width)
    swaps = [
        remote(pack.at[core], pack.at[core], pair_send.at[0], pair_recv.at[0], (partner, e)),
        remote(wg_h.at[0], wg_v.at[core, mine], pair_send.at[1], pair_recv.at[1], (partner, e)),
        remote(wu_h.at[0], wu_v.at[core, mine], pair_send.at[2], pair_recv.at[2], (partner, e)),
        remote(wd_h.at[0], wd_v.at[core, mine], pair_send.at[3], pair_recv.at[3], (partner, e)),
    ]
    for one in swaps:
        one.start()

    drain(r1.at[pl.ds(0, nc - 1)], rsem.at[0])
    stats = r1[:, :, hl:].astype(F32)
    peaks = stats[:, 0:8]
    factor = jnp.exp(peaks - jnp.max(peaks, axis=0)[None])
    denom = jnp.sum(factor * stats[:, 8:16], axis=0)
    denom = denom[:, 0:1] + denom[:, 64:65]
    columns = []
    for top in range(2):
        for a in range(0, hl, WIDE):
            block = r1[:, :, a : a + WIDE].astype(F32)[:, 8 * top : 8 * top + 8]
            columns.append(jnp.sum(factor * block, axis=0))
    latent = (jnp.concatenate(columns, axis=1) / denom).astype(BF16)

    loads[7].wait()
    first = jnp.dot(latent, wuv_v[0], preferred_element_type=F32)
    second = jnp.dot(latent, wuv_v[1], preferred_element_type=F32)
    upper = iota((8, WIDE), 0) < 4
    lane = iota((8, WIDE), 1)
    values = jnp.concatenate(
        [
            jnp.where(upper, first, pltpu.roll(first, 4, 0)),
            jnp.where(upper, pltpu.roll(second, 4, 0), second),
        ],
        axis=1,
    ).astype(BF16)
    loads[8].wait()
    group = min(4, nk)
    for g in range(0, nk, group):
        begin, size = 2 * width * g, 2 * width * group
        part = jnp.dot(values, wout_v[:, begin : begin + size], preferred_element_type=F32)
        part = jnp.concatenate([part, jnp.zeros((8, WIDE), F32)], axis=1)
        for i in range(group):
            a = 2 * width * i
            s2[g + i] = jnp.where(upper, part[:, a : a + WIDE], part[:, a + width : a + width + WIDE])

    def send_2(d):
        remote(s2.at[d], r2.at[c], ssem.at[1], rsem.at[1], (2 * d + side, e)).start()

    for offset in chips:
        send_2(chip_at(offset))

    @pl.when(owner)
    def _():
        r2[pl.ds(c, 1)] = s2[pl.ds(k, 1)]

    @pl.when(jnp.logical_not(owner))
    def _():
        send_2(k)

    swaps[0].wait_recv()

    @pl.when(owner)
    def _():
        drain(r2.at[pl.ds(0, nc - 1)], rsem.at[1])
        stream = jnp.sum(r2[...], axis=0) + jnp.where(upper, pack[0, 0:8], pack[1, 0:8])
        stream = jnp.where(lane < width, stream, 0.0)
        hidden = stream.astype(BF16).astype(F32)
        hid_v[...] = hidden
        st_v[...] = stream
        r3[pl.ds(lax.rem(e, half), 1)] = hidden[None]


        @pl.when(place < ne - 1)
        def _():
            pl.semaphore_wait(hello, ne - 1 - place)

        for i in far:
            z = lax.rem(e + i, ne)
            remote(hid_v, r3.at[lax.rem(e, half)], ssem.at[2], rsem.at[2], (c, z)).start()
        remote(st_v, st_v, pair_send.at[4], pair_recv.at[4], (partner, e)).start()
        drain(r3.at[pl.ds(0, half - 1)], rsem.at[2])

    @pl.when(jnp.logical_not(owner))
    def _():
        drain(r3, rsem.at[2])

    got = r3[...]
    turned = pltpu.roll(got, 4, 1)
    top3 = iota((half // 2, 8, WIDE), 1) < 4
    got, turned = got.reshape(half // 2, 2, 8, WIDE), turned.reshape(half // 2, 2, 8, WIDE)
    tokens = [
        jnp.where(top3, got[:, 0], turned[:, 1]).reshape(batch, WIDE),
        jnp.where(top3, turned[:, 0], got[:, 1]).reshape(batch, WIDE),
    ]
    squares = jnp.sum(tokens[0] * tokens[0] + tokens[1] * tokens[1], axis=1, keepdims=True)
    scaled = [(tokens[f] * pack[f, 8:9, :]).astype(BF16) for f in range(2)]
    logits = jnp.sum(
        scaled[0].astype(F32) * pack[0, 9:10, :] + scaled[1].astype(F32) * pack[1, 9:10, :],
        axis=1,
        keepdims=True,
    )
    scaled = jnp.concatenate(scaled, axis=1)

    lane16 = iota((16, WIDE), 1)
    block = jnp.zeros((16, WIDE), F32)
    lane_at = 0
    for stat in (squares, logits):
        for piece in split_two(stat):
            for a in range(0, batch, 16):
                block = jnp.where(lane16 == lane_at, piece[a : a + 16], block)
                lane_at += 1
    block = block.astype(BF16)
    for n in (9, 10):
        loads[n].wait()
        swaps[n - 8].wait_recv()
    gate = jnp.dot(scaled, wg_v[...].reshape(2 * WIDE, -1), preferred_element_type=F32).astype(BF16)
    up = jnp.dot(scaled, wu_v[...].reshape(2 * WIDE, -1), preferred_element_type=F32).astype(BF16)
    for d in range(nk):
        s4[d, 0:batch] = gate[:, d * WIDE : (d + 1) * WIDE]
        s4[d, batch : 2 * batch] = up[:, d * WIDE : (d + 1) * WIDE]
        s4[d, 2 * batch :] = block
    r4[pl.ds(k, 1)] = s4[pl.ds(k, 1)]

    for offset in chips:
        d = chip_at(offset)
        remote(s4.at[d], r4.at[k], ssem.at[3], rsem.at[3], (2 * d + core, e)).start()

    drain(r4.at[pl.ds(0, nk - 1)], rsem.at[3])
    sums = jnp.sum(r4[...].astype(F32), axis=0)
    gate, up, block = sums[0:batch], sums[batch : 2 * batch], sums[2 * batch :]
    parts = batch // 16

    def column(n):
        pair = block[:, n * parts : (n + 1) * parts] + block[:, (n + 1) * parts : (n + 2) * parts]
        return jnp.concatenate([pair[:, a : a + 1] for a in range(parts)], axis=0)

    inverse = lax.rsqrt(column(0) / (width * nc) + EPS)
    score = jax.nn.sigmoid(column(2) * inverse).astype(BF16).astype(F32)
    gate = gate * inverse
    act = gate / (1.0 + jnp.exp(-gate)) * (up * inverse) * score
    act = act.astype(BF16)

    s5[...] = act
    r5[pl.ds(k, 1)] = act[None]

    for offset in chips:
        d = chip_at(offset)
        remote(s5, r5.at[k], ssem.at[4], rsem.at[4], (2 * d + core, e)).start()

    loads[11].wait()
    swaps[3].wait_recv()
    drain(r5.at[pl.ds(0, nk - 1)], rsem.at[4])
    act = jnp.concatenate([r5[d] for d in range(nk)], axis=1)
    made = lax.dot_general(
        act, wd_v[...].reshape(2 * WIDE, -1), (((1,), (1,)), ((), ())), preferred_element_type=F32
    )
    shown = iota((batch, WIDE), 1) >= width
    for f in range(2):
        s6[f] = jnp.where(shown, score, made[:, f * WIDE : (f + 1) * WIDE]).reshape(half, 4, WIDE)

    def send_6(t, f):
        remote(s6.at[f, t], r6.at[e], ssem.at[5], rsem.at[5], (2 * k + f, half * core + t)).start()

    turn = lax.rem(e, half)
    for i in range(half):
        t = lax.rem(turn + (half // 2 + i), half)
        for f in range(2):
            if i == half // 2:
                pl.when(jnp.logical_not(owner & (core == f)))(functools.partial(send_6, t, f))
            else:
                send_6(t, f)

    @pl.when(owner)
    def _():
        r6[pl.ds(e, 1)] = s6[core, pl.ds(turn, 1)]
        drain(r6.at[pl.ds(0, ne - 1)], rsem.at[5])

    @pl.when(jnp.logical_not(owner))
    def _():
        drain(r6, rsem.at[5])
        pltpu.make_async_copy(st_v, st_v, pair_recv.at[4]).wait()

    mixed = jnp.sum(jnp.where(hit_v[...] > 0.0, r6[...], 0.0), axis=0)
    stream = st_v[...]
    stream = jnp.where(core == 1, pltpu.roll(stream, 4, 0), stream)[0:4]
    out_ref[...] = stream[:, 0:width] + ROUTE * mixed[:, 0:width] / mixed[:, width : width + 1]

    drain(s1.at[pl.ds(0, nc - 1)], ssem.at[0])
    drain(s2.at[pl.ds(0, nk - 1)], ssem.at[1])
    drain(s4.at[pl.ds(0, nk - 1)], ssem.at[3])
    drain(r5.at[pl.ds(0, nk - 1)], ssem.at[4])
    drain(r6.at[pl.ds(0, ne - 1)], ssem.at[5])

    @pl.when(owner)
    def _():
        for _ in far:
            drain(hid_v, ssem.at[2])
        pltpu.make_async_copy(st_v, st_v, pair_send.at[4]).wait()

    @pl.when(jnp.logical_not(owner))
    def _():
        drain(s2.at[0], ssem.at[1])
        drain(r6.at[0], ssem.at[5])

    for one in swaps:
        one.wait_send()


def per_device(nc, ne, *args):
    (queries, cache, lengths, w_uv, w_out, residual, gain, router, w_gate, w_up, w_down, ids) = args
    nk, half = nc // 2, ne // 2
    width, ff = w_gate.shape[1], w_gate.shape[2]
    batch = 4 * half
    hbm = pl.BlockSpec(memory_space=pltpu.HBM)
    vmem = lambda *shape, dtype=F32: pltpu.VMEM(shape, dtype)
    half_type = functools.partial(vmem, dtype=BF16)
    like = lambda x: pltpu.VMEM(x.shape, x.dtype)
    gain = gain.reshape(1, width)
    w_down = jnp.swapaxes(w_down, 1, 2)
    scratch = [
        like(queries), like(cache), pltpu.SMEM(lengths.shape, I32), like(w_uv), like(w_out), like(residual),
        like(gain), like(router),
        half_type(2, WIDE, ff), half_type(2, WIDE, ff), half_type(2, WIDE, ff), like(ids),
        vmem(2, 16, WIDE), vmem(ne, 4, WIDE), vmem(8, WIDE), vmem(8, WIDE),
        half_type(nc, 16, LATENT // 2 + WIDE), half_type(nc, 16, LATENT // 2 + WIDE),
        vmem(nk, 8, WIDE), vmem(nc, 8, WIDE),
        vmem(half, 8, WIDE),
        half_type(nk, 2 * batch + 16, WIDE), half_type(nk, 2 * batch + 16, WIDE),
        half_type(batch, WIDE), half_type(nk, batch, WIDE),
        vmem(2, half, 4, WIDE), vmem(ne, 4, WIDE),
        pltpu.SemaphoreType.DMA((12,)),
        pltpu.SemaphoreType.DMA((5,)), pltpu.SemaphoreType.DMA((5,)),
        pltpu.SemaphoreType.DMA((6,)), pltpu.SemaphoreType.DMA((6,)), pltpu.SemaphoreType.REGULAR,
    ]
    return pl.pallas_call(
        functools.partial(kernel, nc, ne),
        out_shape=jax.ShapeDtypeStruct((4, width), F32),
        in_specs=[hbm] * 12,
        out_specs=pl.BlockSpec(memory_space=pltpu.VMEM),
        scratch_shapes=scratch,
        compiler_params=pltpu.CompilerParams(
            collective_id=0, has_side_effects=True, vmem_limit_bytes=64 * 1024 * 1024
        ),
    )(queries, cache, lengths, w_uv, w_out, residual, gain, router, w_gate, w_up, w_down, ids)


def solution(mesh):
    in_specs = (
        P("ep", None, None),
        P("ep", "ctx", None),
        P("ep"),
        P("ctx", None, None),
        P("ctx", None),
        P("ep", "ctx"),
        P("ctx"),
        P("ep", "ctx"),
        P("ep", "ctx", None),
        P("ep", "ctx", None),
        P("ep", None, "ctx"),
        P("ep", None),
    )
    return jax.shard_map(
        functools.partial(per_device, mesh.shape["ctx"], mesh.shape["ep"]),
        mesh=mesh, in_specs=in_specs, out_specs=P("ep", "ctx"), check_vma=False,
    )
```

```python
import functools

import jax
import jax.numpy as jnp
from jax import lax
from jax.experimental import pallas as pl
from jax.experimental.pallas import tpu as pltpu
from jax.sharding import PartitionSpec as P

SCALE = 192.0 ** (-0.5)
FLOOR = -1e30
EPS = 1e-06
ROUTE = 2.5
LATENT = 512
WIDE = 128
MESH = pl.DeviceIdType.MESH
BF16, F32, I32 = jnp.bfloat16, jnp.float32, jnp.int32


def iota(shape, dim):
    return lax.broadcasted_iota(I32, shape, dim)


def split_two(x):
    high = x.astype(BF16).astype(F32)
    return high, x - high


def kernel(
    nc,
    ne,
    q_h, cache_h, len_h, wuv_h, wout_h, res_h, gain_h, router_h, wg_h, wu_h, wd_h, ids_h,
    out_ref,
    q_v, cache_v, len_s, wuv_v, wout_v, res_v, gain_v, router_v, wg_v, wu_v, wd_v, ids_v,
    pack, hit_v, st_v, hid_v,
    s1, p1, own_v, own_peak, own_total, m1, r1, s2, r2, r3, s4, r4, s5, r5, score_v, s6, r6,
    load_sem, pair_send, pair_recv, ssem, rsem, hello,
):
    nk, half = nc // 2, ne // 2
    width = res_h.shape[1]
    span = cache_h.shape[1]
    rows = 8 * nc
    split = half // 2
    batch = 4 * split
    c, e = lax.axis_index("ctx"), lax.axis_index("ep")
    k, core = c // 2, lax.rem(c, 2)
    side = e // half
    turn = lax.rem(e, half)
    mine_in = turn // split
    owner = core == side
    partner = 2 * k + 1 - core

    def load(n, src, dst):
        return pltpu.make_async_copy(src, dst, load_sem.at[n])

    loads = [
        load(0, q_h, q_v),
        load(1, cache_h, cache_v),
        load(2, len_h, len_s),
        load(3, res_h, res_v),
        load(4, gain_h, gain_v),
        load(5, router_h, router_v),
        load(6, ids_h, ids_v),
        load(7, wuv_h, wuv_v),
        load(8, wout_h, wout_v),
        load(9, wg_h.at[0], wg_v.at[core, pl.ds(0, width)]),
        load(10, wu_h.at[0], wu_v.at[core, pl.ds(0, width)]),
        load(11, wd_h.at[0], wd_v.at[core, pl.ds(0, width)]),
    ]
    for one in loads:
        one.start()

    place = jnp.where((core == 1) & (e >= half), ne - 1 - (e - half), e)
    base = core * half
    source = (place >= base) & (place < base + half)

    def at_place(p):
        return (c, jnp.where((core == 1) & (p >= half), ne - 1 - (p - half), p))

    xs = 4 if nk % 4 == 0 else nk
    ys = nk // xs
    hops = lambda o: min(o[0], ys - o[0]) + min(o[1], xs - o[1])
    chips = [(dy, dx) for dy in range(ys) for dx in range(xs) if (dy, dx) != (0, 0)]
    chips.sort(key=lambda o: -hops(o))
    remotes = len([o for o in chips if hops(o) > 2])
    here = len(chips)

    def chip_at(offset):
        return lax.rem(k // xs + offset[0], ys) * xs + lax.rem(k + offset[1], xs)

    barrier = pltpu.get_barrier_semaphore()

    def greet(to):
        pl.semaphore_signal(barrier, inc=1, device_id=to, device_id_type=MESH)

    for offset in chips:
        greet((2 * chip_at(offset) + core, e))
    greet((partner, e))

    def greet_ep(p, _):
        greet(at_place(p))
        return 0

    first_up = jnp.where(core == 0, jnp.where(source, place + 1, ne), jnp.maximum(place + 1, half))
    lax.fori_loop(first_up, ne, greet_ep, 0)
    greeted = jnp.where(core == 0, jnp.minimum(place, half), jnp.where(source, place, 0))

    def answer(p, _):
        pl.semaphore_signal(hello, inc=1, device_id=at_place(p), device_id_type=MESH)
        return 0

    far = sorted(range(1, ne), key=lambda i: -min(i, ne - i))

    def remote(src, dst, send, recv, to):
        return pltpu.make_async_remote_copy(
            src_ref=src, dst_ref=dst, send_sem=send, recv_sem=recv, device_id=to, device_id_type=MESH
        )

    def drain(ref, sem):
        pltpu.make_async_copy(ref, ref, sem).wait()

    for one in loads[2:7]:
        one.wait()
    pack[pl.ds(core, 1)] = jnp.zeros((1, 16, WIDE), F32)
    wide_res = res_v[...].astype(F32)
    pack[core, 0:8, 0:width] = jnp.concatenate([wide_res, wide_res], axis=0)
    pack[core, 8:9, 0:width] = gain_v[...]
    pack[core, 9:10, 0:width] = router_v[...].astype(F32)
    blank = jnp.zeros((2, WIDE - width, wg_v.shape[2]), BF16)
    wg_v[:, width:WIDE, :] = blank
    wu_v[:, width:WIDE, :] = blank
    wd_v[:, width:WIDE, :] = blank
    ids = ids_v[...]
    for x in range(ne):
        hit = jnp.max(jnp.where(ids == x, 1.0, 0.0), axis=1, keepdims=True)
        hit_v[x] = jnp.broadcast_to(hit, (4, WIDE))

    loads[0].wait()
    row = iota((rows, rows), 0)
    other = row >= 8 * nk
    want = (row & 3) * (2 * nc) + 4 * ((row >> 3) - jnp.where(other, nk, 0)) + ((row >> 2) & 1)
    want = want + 2 * jnp.where(other, 1 - core, core)
    order = jnp.where(iota((rows, rows), 1) == want, 1.0, 0.0).astype(BF16)
    q = q_v[...].reshape(rows, q_v.shape[2])
    q = jnp.dot(order, q, preferred_element_type=F32).astype(BF16)
    loads[1].wait()
    keys = cache_v[...].reshape(4 * span, cache_v.shape[2])
    scores = lax.dot_general(q, keys, (((1,), (1,)), ((), ())), preferred_element_type=F32) * SCALE
    col = iota((1, 4 * span), 1)
    col_row = jnp.zeros_like(col)
    limit = jnp.full_like(col, len_s[0])
    for r in range(1, 4):
        past = col >= r * span
        col_row = jnp.where(past, r, col_row)
        limit = jnp.where(past, len_s[r], limit)
    position = c * span + col - col_row * span
    col_row = jnp.where(position < limit, col_row, -1)
    valid = (iota((rows, 4 * span), 0) & 3) == col_row
    masked = jnp.where(valid, scores, FLOOR)
    peak = jnp.max(masked, axis=1, keepdims=True).astype(BF16).astype(F32)
    weights = jnp.where(valid, jnp.exp(masked - peak), 0.0).astype(BF16)
    total = jnp.sum(weights.astype(F32), axis=1, keepdims=True)
    summed = jnp.dot(weights, keys[:, :LATENT], preferred_element_type=F32)
    summed = summed.reshape(2, nk, 8, LATENT)
    hl = LATENT // 2
    chunks = range(0, hl, WIDE)
    peaks = jnp.broadcast_to(peak, (rows, WIDE)).reshape(2, nk, 8, WIDE)
    totals = jnp.broadcast_to(total, (rows, WIDE)).reshape(2, nk, 8, WIDE)
    side_lane = iota((nk, 8, WIDE), 2) < 64

    def put(ref, top, amount, parts):
        high, rest = split_two(amount)
        for n, a in enumerate(chunks):
            ref[:, :, a : a + WIDE] = jnp.concatenate([parts[n], parts[n + len(chunks)]], axis=1).astype(BF16)
        ref[:, :, hl:] = jnp.concatenate([top, jnp.where(side_lane, high, rest)], axis=1).astype(BF16)

    columns = range(0, LATENT, WIDE)
    put(s1, peaks[1], totals[1], [summed[1, :, :, a : a + WIDE] for a in columns])
    own_v[...] = summed[0]
    own_peak[...] = peaks[0]
    own_total[...] = totals[0]

    pl.semaphore_wait(barrier, nk + greeted)
    lax.fori_loop(base, jnp.where(source | (core == 0), jnp.minimum(place, base + half), base), answer, 0)

    swap = remote(s1, p1, pair_send.at[5], pair_recv.at[5], (partner, e))
    swap.start()

    mine = pl.ds(0, width)
    swaps = [
        remote(pack.at[core], pack.at[core], pair_send.at[0], pair_recv.at[0], (partner, e)),
        remote(wg_h.at[0], wg_v.at[core, mine], pair_send.at[1], pair_recv.at[1], (partner, e)),
        remote(wu_h.at[0], wu_v.at[core, mine], pair_send.at[2], pair_recv.at[2], (partner, e)),
        remote(wd_h.at[0], wd_v.at[core, mine], pair_send.at[3], pair_recv.at[3], (partner, e)),
    ]
    swap.wait_recv()

    def stats_of(x):
        x = x.astype(F32)
        return x[:, 0:8], x[:, 8:16]

    peaks, totals = stats_of(p1[:, :, hl:])
    totals = totals + pltpu.roll(totals, 64, 2)
    top = jnp.maximum(peaks, own_peak[...])
    from_own, from_other = jnp.exp(own_peak[...] - top), jnp.exp(peaks - top)
    lefts, rights = [], []
    for a in chunks:
        block = p1[:, :, a : a + WIDE].astype(F32)
        lefts.append(from_own * own_v[:, :, a : a + WIDE] + from_other * block[:, 0:8])
        rights.append(from_own * own_v[:, :, hl + a : hl + a + WIDE] + from_other * block[:, 8:16])
    put(m1, top, from_own * own_total[...] + from_other * totals, lefts + rights)
    r1[here] = m1[k]
    for n, offset in enumerate(chips):
        d = chip_at(offset)
        remote(m1.at[d], r1.at[n], ssem.at[0], rsem.at[0], (2 * d + core, e)).start()
    for one in swaps:
        one.start()

    drain(r1.at[pl.ds(0, here)], rsem.at[0])
    peaks, totals = stats_of(r1[:, :, hl:])
    factor = jnp.exp(peaks - jnp.max(peaks, axis=0)[None])
    denom = jnp.sum(factor * totals, axis=0)
    denom = denom[:, 0:1] + denom[:, 64:65]
    columns = []
    for first in (0, 8):
        for a in chunks:
            block = r1[:, :, a : a + WIDE].astype(F32)[:, first : first + 8]
            columns.append(jnp.sum(factor * block, axis=0))
    latent = (jnp.concatenate(columns, axis=1) / denom).astype(BF16)

    loads[7].wait()
    first = jnp.dot(latent, wuv_v[0], preferred_element_type=F32)
    second = jnp.dot(latent, wuv_v[1], preferred_element_type=F32)
    upper = iota((8, WIDE), 0) < 4
    lane = iota((8, WIDE), 1)
    values = jnp.concatenate(
        [
            jnp.where(upper, first, pltpu.roll(first, 4, 0)),
            jnp.where(upper, pltpu.roll(second, 4, 0), second),
        ],
        axis=1,
    ).astype(BF16)
    loads[8].wait()
    group = min(4, nk)
    for g in range(0, nk, group):
        begin, size = 2 * width * g, 2 * width * group
        part = jnp.dot(values, wout_v[:, begin : begin + size], preferred_element_type=F32)
        part = jnp.concatenate([part, jnp.zeros((8, WIDE), F32)], axis=1)
        for i in range(group):
            a = 2 * width * i
            s2[g + i] = jnp.where(upper, part[:, a : a + WIDE], part[:, a + width : a + width + WIDE])

    def send_2(n, d, sem):
        remote(s2.at[d], r2.at[2 * n + core], ssem.at[1], rsem.at[sem], (2 * d + side, e)).start()

    for n, offset in enumerate(chips):
        send_2(n, chip_at(offset), 7 if n < remotes else 1)

    @pl.when(owner)
    def _():
        r2[2 * here + core] = s2[k]

    @pl.when(jnp.logical_not(owner))
    def _():
        send_2(here, k, 1)

    swaps[0].wait_recv()

    @pl.when(owner)
    def _():
        drain(r2.at[pl.ds(0, 2 * (here - remotes) + 1)], rsem.at[1])
        stream = jnp.where(upper, pack[0, 0:8], pack[1, 0:8])
        stream = stream + jnp.sum(r2[2 * remotes :], axis=0)
        if remotes:
            drain(r2.at[pl.ds(0, 2 * remotes)], rsem.at[7])
            stream = stream + jnp.sum(r2[0 : 2 * remotes], axis=0)
        stream = jnp.where(lane < width, stream, 0.0)
        hidden = stream.astype(BF16).astype(F32)
        hid_v[...] = hidden
        st_v[...] = stream
        r3[pl.ds(turn, 1)] = hidden[None]


        @pl.when(place < ne - 1)
        def _():
            pl.semaphore_wait(hello, ne - 1 - place)

        arrived = rsem.at[2 + mine_in]
        for i in far:
            z = lax.rem(e + i, ne)
            remote(hid_v, r3.at[turn], ssem.at[2], arrived, (c, z)).start()
        remote(st_v, st_v, pair_send.at[4], pair_recv.at[4], (partner, e)).start()

    def wait_3(b):
        here_too = owner & (mine_in == b)
        pl.when(here_too)(lambda: drain(r3.at[pl.ds(0, split - 1)], rsem.at[2 + b]))
        pl.when(jnp.logical_not(here_too))(lambda: drain(r3.at[pl.ds(0, split)], rsem.at[2 + b]))

    def send_4(b):
        got = r3[b * split : (b + 1) * split]
        turned = pltpu.roll(got, 4, 1)
        pairs = (split // 2, 2, 8, WIDE)
        top3 = iota((split // 2, 8, WIDE), 1) < 4
        got, turned = got.reshape(pairs), turned.reshape(pairs)
        tokens = [
            jnp.where(top3, got[:, 0], turned[:, 1]).reshape(batch, WIDE),
            jnp.where(top3, turned[:, 0], got[:, 1]).reshape(batch, WIDE),
        ]
        squares = jnp.sum(tokens[0] * tokens[0] + tokens[1] * tokens[1], axis=1, keepdims=True)
        scaled = [(tokens[f] * pack[f, 8:9, :]).astype(BF16) for f in range(2)]
        logits = jnp.sum(
            scaled[0].astype(F32) * pack[0, 9:10, :] + scaled[1].astype(F32) * pack[1, 9:10, :],
            axis=1,
            keepdims=True,
        )
        scaled = jnp.concatenate(scaled, axis=1)
        lane16 = iota((16, WIDE), 1)
        block = jnp.zeros((16, WIDE), F32)
        lane_at = 0
        for stat in (squares, logits):
            for piece in split_two(stat):
                for a in range(0, batch, 16):
                    block = jnp.where(lane16 == lane_at, piece[a : a + 16], block)
                    lane_at += 1
        block = block.astype(BF16)
        gate = jnp.dot(scaled, wg_v[...].reshape(2 * WIDE, -1), preferred_element_type=F32).astype(BF16)
        up = jnp.dot(scaled, wu_v[...].reshape(2 * WIDE, -1), preferred_element_type=F32).astype(BF16)
        for d in range(nk):
            s4[b, d, 0:batch] = gate[:, d * WIDE : (d + 1) * WIDE]
            s4[b, d, batch : 2 * batch] = up[:, d * WIDE : (d + 1) * WIDE]
            s4[b, d, 2 * batch :] = block
        r4[b, here] = s4[b, k]
        for n, offset in enumerate(chips):
            d = chip_at(offset)
            sem = rsem.at[(10 if n < remotes else 8) + b]
            remote(s4.at[b, d], r4.at[b, n], ssem.at[3], sem, (2 * d + core, e)).start()

    def send_5(b):
        drain(r4.at[b, pl.ds(0, here - remotes)], rsem.at[8 + b])
        sums = jnp.sum(r4[b, remotes:].astype(F32), axis=0)
        if remotes:
            drain(r4.at[b, pl.ds(0, remotes)], rsem.at[10 + b])
            sums = sums + jnp.sum(r4[b, 0:remotes].astype(F32), axis=0)
        gate, up, block = sums[0:batch], sums[batch : 2 * batch], sums[2 * batch :]
        parts = batch // 16

        def column(n):
            n = n * parts
            pair = block[:, n : n + parts] + block[:, n + parts : n + 2 * parts]
            return jnp.concatenate([pair[:, a : a + 1] for a in range(parts)], axis=0)

        inverse = lax.rsqrt(column(0) / (width * nc) + EPS)
        score = jax.nn.sigmoid(column(2) * inverse).astype(BF16).astype(F32)
        gate = gate * inverse
        act = gate / (1.0 + jnp.exp(-gate)) * (up * inverse) * score
        act = act.astype(BF16)
        s5[b] = act
        score_v[b] = jnp.broadcast_to(score, (batch, WIDE))
        r5[b, pl.ds(k, 1)] = act[None]
        for offset in chips:
            d = chip_at(offset)
            remote(s5.at[b], r5.at[b, k], ssem.at[4], rsem.at[12 + b], (2 * d + core, e)).start()

    def send_6(b):
        drain(r5.at[b, pl.ds(0, nk - 1)], rsem.at[12 + b])
        act = jnp.concatenate([r5[b, d] for d in range(nk)], axis=1)
        made = lax.dot_general(
            act, wd_v[...].reshape(2 * WIDE, -1), (((1,), (1,)), ((), ())), preferred_element_type=F32
        )
        shown = iota((batch, WIDE), 1) >= width
        for f in range(2):
            block = jnp.where(shown, score_v[b], made[:, f * WIDE : (f + 1) * WIDE])
            s6[f, b * split : (b + 1) * split] = block.reshape(split, 4, WIDE)

        def back(t, f):
            remote(s6.at[f, t], r6.at[e], ssem.at[5], rsem.at[5], (2 * k + f, half * core + t)).start()

        for i in range(1, split + 1):
            t = b * split + lax.rem(turn + i, split)
            for f in range(2):
                if i == split:
                    pl.when(jnp.logical_not(owner & (core == f) & (mine_in == b)))(functools.partial(back, t, f))
                else:
                    back(t, f)

    wait_3(0)
    for n in (9, 10):
        loads[n].wait()
        swaps[n - 8].wait_recv()
    send_4(0)
    wait_3(1)
    send_4(1)
    send_5(0)
    send_5(1)
    loads[11].wait()
    swaps[3].wait_recv()
    send_6(0)
    send_6(1)

    @pl.when(owner)
    def _():
        r6[pl.ds(e, 1)] = s6[core, pl.ds(turn, 1)]
        drain(r6.at[pl.ds(0, ne - 1)], rsem.at[5])

    @pl.when(jnp.logical_not(owner))
    def _():
        drain(r6, rsem.at[5])
        pltpu.make_async_copy(st_v, st_v, pair_recv.at[4]).wait()

    mixed = jnp.sum(jnp.where(hit_v[...] > 0.0, r6[...], 0.0), axis=0)
    stream = st_v[...]
    stream = jnp.where(core == 1, pltpu.roll(stream, 4, 0), stream)[0:4]
    out_ref[...] = stream[:, 0:width] + ROUTE * mixed[:, 0:width] / mixed[:, width : width + 1]

    swap.wait_send()
    drain(s1.at[pl.ds(0, nk - 1)], ssem.at[0])
    drain(s2.at[pl.ds(0, nk - 1)], ssem.at[1])
    for b in range(2):
        drain(s4.at[b, pl.ds(0, nk - 1)], ssem.at[3])
        drain(r5.at[b, pl.ds(0, nk - 1)], ssem.at[4])
    drain(r6.at[pl.ds(0, ne - 1)], ssem.at[5])

    @pl.when(owner)
    def _():
        for _ in far:
            drain(hid_v, ssem.at[2])
        pltpu.make_async_copy(st_v, st_v, pair_send.at[4]).wait()

    @pl.when(jnp.logical_not(owner))
    def _():
        drain(s2.at[0], ssem.at[1])
        drain(r6.at[0], ssem.at[5])

    for one in swaps:
        one.wait_send()


def per_device(nc, ne, *args):
    (queries, cache, lengths, w_uv, w_out, residual, gain, router, w_gate, w_up, w_down, ids) = args
    nk, half = nc // 2, ne // 2
    width, ff = w_gate.shape[1], w_gate.shape[2]
    split = half // 2
    batch = 4 * split
    hbm = pl.BlockSpec(memory_space=pltpu.HBM)
    vmem = lambda *shape, dtype=F32: pltpu.VMEM(shape, dtype)
    half_type = functools.partial(vmem, dtype=BF16)
    like = lambda x: pltpu.VMEM(x.shape, x.dtype)
    gain = gain.reshape(1, width)
    w_down = jnp.swapaxes(w_down, 1, 2)
    scratch = [
        like(queries), like(cache), pltpu.SMEM(lengths.shape, I32), like(w_uv), like(w_out), like(residual),
        like(gain), like(router),
        half_type(2, WIDE, ff), half_type(2, WIDE, ff), half_type(2, WIDE, ff), like(ids),
        vmem(2, 16, WIDE), vmem(ne, 4, WIDE), vmem(8, WIDE), vmem(8, WIDE),
        half_type(nk, 16, LATENT // 2 + WIDE), half_type(nk, 16, LATENT // 2 + WIDE),
        vmem(nk, 8, LATENT), vmem(nk, 8, WIDE), vmem(nk, 8, WIDE),
        half_type(nk, 16, LATENT // 2 + WIDE), half_type(nk, 16, LATENT // 2 + WIDE),
        vmem(nk, 8, WIDE), vmem(nc, 8, WIDE),
        vmem(half, 8, WIDE),
        half_type(2, nk, 2 * batch + 16, WIDE), half_type(2, nk, 2 * batch + 16, WIDE),
        half_type(2, batch, WIDE), half_type(2, nk, batch, WIDE), vmem(2, batch, WIDE),
        vmem(2, half, 4, WIDE), vmem(ne, 4, WIDE),
        pltpu.SemaphoreType.DMA((12,)),
        pltpu.SemaphoreType.DMA((6,)), pltpu.SemaphoreType.DMA((6,)),
        pltpu.SemaphoreType.DMA((6,)), pltpu.SemaphoreType.DMA((14,)), pltpu.SemaphoreType.REGULAR,
    ]
    return pl.pallas_call(
        functools.partial(kernel, nc, ne),
        out_shape=jax.ShapeDtypeStruct((4, width), F32),
        in_specs=[hbm] * 12,
        out_specs=pl.BlockSpec(memory_space=pltpu.VMEM),
        scratch_shapes=scratch,
        compiler_params=pltpu.CompilerParams(
            collective_id=0, has_side_effects=True, vmem_limit_bytes=64 * 1024 * 1024
        ),
    )(queries, cache, lengths, w_uv, w_out, residual, gain, router, w_gate, w_up, w_down, ids)


def solution(mesh):
    in_specs = (
        P("ep", None, None),
        P("ep", "ctx", None),
        P("ep"),
        P("ctx", None, None),
        P("ctx", None),
        P("ep", "ctx"),
        P("ctx"),
        P("ep", "ctx"),
        P("ep", "ctx", None),
        P("ep", "ctx", None),
        P("ep", None, "ctx"),
        P("ep", None),
    )
    return jax.shard_map(
        functools.partial(per_device, mesh.shape["ctx"], mesh.shape["ep"]),
        mesh=mesh, in_specs=in_specs, out_specs=P("ep", "ctx"), check_vma=False,
    )
```

```python
import functools

import jax
import jax.numpy as jnp
from jax import lax
from jax.experimental import pallas as pl
from jax.experimental.pallas import tpu as pltpu
from jax.sharding import PartitionSpec as P

SCALE = 192.0 ** (-0.5)
FLOOR = -1e30
EPS = 1e-06
ROUTE = 2.5
LATENT = 512
WIDE = 128
MESH = pl.DeviceIdType.MESH
BF16, F32, I32 = jnp.bfloat16, jnp.float32, jnp.int32


def iota(shape, dim):
    return lax.broadcasted_iota(I32, shape, dim)


def split_two(x):
    high = x.astype(BF16).astype(F32)
    return high, x - high


def kernel(
    nc,
    ne,
    q_h, cache_h, len_h, wuv_h, wout_h, res_h, gain_h, router_h, wg_h, wu_h, wd_h, ids_h,
    out_ref,
    q_v, cache_v, len_s, wuv_v, wout_v, res_v, gain_v, router_v, wg_v, wu_v, wd_v, ids_v,
    pack, hit_v, st_v, hid_v,
    s1, p1, own_v, own_peak, own_total, m1, r1, s2, r2, r3, s4, r4, s5, r5, score_v, s6, r6,
    load_sem, pair_send, pair_recv, ssem, rsem, hello, known,
):
    nk, half = nc // 2, ne // 2
    width = res_h.shape[1]
    span = cache_h.shape[1]
    rows = 8 * nc
    split = half // 2
    batch = 4 * split
    c, e = lax.axis_index("ctx"), lax.axis_index("ep")
    k, core = c >> 1, c & 1
    side = e // half
    turn = e & (half - 1)
    mine_in = turn // split
    owner = core == side
    partner = 2 * k + 1 - core

    def load(n, src, dst):
        return pltpu.make_async_copy(src, dst, load_sem.at[n])

    loads = [
        load(0, q_h, q_v),
        load(1, cache_h, cache_v),
        load(2, len_h, len_s),
        load(3, res_h, res_v),
        load(4, gain_h, gain_v),
        load(5, router_h, router_v),
        load(6, ids_h, ids_v),
        load(7, wuv_h, wuv_v),
        load(8, wout_h, wout_v),
        load(9, wg_h.at[0], wg_v.at[core, pl.ds(0, width)]),
        load(10, wu_h.at[0], wu_v.at[core, pl.ds(0, width)]),
        load(11, wd_h.at[0], wd_v.at[core, pl.ds(0, width)]),
    ]
    for one in loads[:3]:
        one.start()

    place = jnp.where((core == 1) & (e >= half), ne - 1 - (e - half), e)
    base = core * half
    source = (place >= base) & (place < base + half)

    def at_place(p):
        return (c, jnp.where((core == 1) & (p >= half), ne - 1 - (p - half), p))

    xs = 4 if nk % 4 == 0 else nk
    ys = nk // xs
    hops = lambda o: min(o[0], ys - o[0]) + min(o[1], xs - o[1])
    chips = [(dy, dx) for dy in range(ys) for dx in range(xs) if (dy, dx) != (0, 0)]
    chips.sort(key=lambda o: -hops(o))
    remotes = len([o for o in chips if hops(o) > 2])
    here = len(chips)

    peers = {o: ((k // xs + o[0]) & (ys - 1)) * xs + ((k + o[1]) & (xs - 1)) for o in chips}

    def chip_at(offset):
        return peers[offset]

    barrier = pltpu.get_barrier_semaphore()

    def greet(to):
        pl.semaphore_signal(barrier, inc=1, device_id=to, device_id_type=MESH)

    for offset in chips:
        greet((2 * chip_at(offset) + side, e))

    @pl.when(owner)
    def _():
        greet((partner, e))

    def greet_ep(p, _):
        z = at_place(p)[1]
        greet((2 * k + jnp.where((core == 0) & (place < split), 0, z // half), z))
        return 0

    first_up = jnp.where(core == 0, jnp.where(source, place + 1, ne), jnp.maximum(place + 1, half))
    lax.fori_loop(first_up, ne, greet_ep, 0)
    greeted = jnp.where(
        owner,
        2 * (nk - 1) + place + jnp.where(core == 1, half - split, 0),
        1 + jnp.where(core == 0, split, 0),
    )

    def answer(p, _):
        pl.semaphore_signal(hello, inc=1, device_id=at_place(p), device_id_type=MESH)
        return 0

    far = sorted(range(1, ne), key=lambda i: -min(i, ne - i))

    def remote(src, dst, send, recv, to):
        return pltpu.make_async_remote_copy(
            src_ref=src, dst_ref=dst, send_sem=send, recv_sem=recv, device_id=to, device_id_type=MESH
        )

    def drain(ref, sem):
        pltpu.make_async_copy(ref, ref, sem).wait()

    for one in loads[3:7]:
        one.start()

    def tell_partner():
        pl.semaphore_signal(known, inc=1, device_id=(partner, e), device_id_type=MESH)

    loads[0].wait()
    row = iota((rows, rows), 0)
    other = row >= 8 * nk
    want = (row & 3) * (2 * nc) + 4 * ((row >> 3) - jnp.where(other, nk, 0)) + ((row >> 2) & 1)
    want = want + 2 * jnp.where(other, 1 - core, core)
    order = jnp.where(iota((rows, rows), 1) == want, 1.0, 0.0).astype(BF16)
    q = q_v[...].reshape(rows, q_v.shape[2])
    q = jnp.dot(order, q, preferred_element_type=F32).astype(BF16)
    loads[1].wait()
    for one in loads[7:]:
        one.start()
    loads[2].wait()
    keys = cache_v[...].reshape(4 * span, cache_v.shape[2])
    scores = lax.dot_general(q, keys, (((1,), (1,)), ((), ())), preferred_element_type=F32) * SCALE
    col = iota((1, 4 * span), 1)
    col_row = jnp.zeros_like(col)
    limit = jnp.full_like(col, len_s[0])
    for r in range(1, 4):
        past = col >= r * span
        col_row = jnp.where(past, r, col_row)
        limit = jnp.where(past, len_s[r], limit)
    position = c * span + col - col_row * span
    col_row = jnp.where(position < limit, col_row, -1)
    valid = (iota((rows, 4 * span), 0) & 3) == col_row
    masked = jnp.where(valid, scores, FLOOR)
    peak = jnp.max(masked, axis=1, keepdims=True).astype(BF16).astype(F32)

    @pl.when(jnp.logical_not(owner))
    def _():
        pl.semaphore_wait(barrier, greeted)
        tell_partner()

        @pl.when(core == 0)
        def _():
            lax.fori_loop(0, split, answer, 0)

    weights = jnp.where(valid, jnp.exp(masked - peak), 0.0).astype(BF16)
    total = jnp.sum(weights.astype(F32), axis=1, keepdims=True)
    summed = jnp.dot(weights, keys[:, :LATENT], preferred_element_type=F32)
    summed = summed.reshape(2, nk, 8, LATENT)
    hl = LATENT // 2
    chunks = range(0, hl, WIDE)
    peaks = jnp.broadcast_to(peak, (rows, WIDE)).reshape(2, nk, 8, WIDE)
    totals = jnp.broadcast_to(total, (rows, WIDE)).reshape(2, nk, 8, WIDE)
    side_lane = iota((nk, 8, WIDE), 2) < 64

    def put(ref, top, amount, parts):
        high, rest = split_two(amount)
        for n, a in enumerate(chunks):
            ref[:, :, a : a + WIDE] = jnp.concatenate([parts[n], parts[n + len(chunks)]], axis=1).astype(BF16)
        ref[:, :, hl:] = jnp.concatenate([top, jnp.where(side_lane, high, rest)], axis=1).astype(BF16)

    columns = range(0, LATENT, WIDE)
    put(s1, peaks[1], totals[1], [summed[1, :, :, a : a + WIDE] for a in columns])
    own_v[...] = summed[0]
    own_peak[...] = peaks[0]
    own_total[...] = totals[0]

    swap = remote(s1, p1, pair_send.at[5], pair_recv.at[5], (partner, e))

    @pl.when(owner)
    def _():
        pl.semaphore_wait(known, 1)
        swap.start()
        pl.semaphore_wait(barrier, greeted)
        tell_partner()
        lax.fori_loop(base, place, answer, 0)

    pl.when(jnp.logical_not(owner))(swap.start)

    mine = pl.ds(0, width)
    swaps = [
        remote(pack.at[core], pack.at[core], pair_send.at[0], pair_recv.at[0], (partner, e)),
        remote(wg_h.at[0], wg_v.at[core, mine], pair_send.at[1], pair_recv.at[1], (partner, e)),
        remote(wu_h.at[0], wu_v.at[core, mine], pair_send.at[2], pair_recv.at[2], (partner, e)),
        remote(wd_h.at[0], wd_v.at[core, mine], pair_send.at[3], pair_recv.at[3], (partner, e)),
    ]
    swap.wait_recv()

    def stats_of(x):
        x = x.astype(F32)
        return x[:, 0:8], x[:, 8:16]

    peaks, totals = stats_of(p1[:, :, hl:])
    totals = totals + pltpu.roll(totals, 64, 2)
    top = jnp.maximum(peaks, own_peak[...])
    from_own, from_other = jnp.exp(own_peak[...] - top), jnp.exp(peaks - top)
    lefts, rights = [], []
    for a in chunks:
        block = p1[:, :, a : a + WIDE].astype(F32)
        lefts.append(from_own * own_v[:, :, a : a + WIDE] + from_other * block[:, 0:8])
        rights.append(from_own * own_v[:, :, hl + a : hl + a + WIDE] + from_other * block[:, 8:16])
    put(m1, top, from_own * own_total[...] + from_other * totals, lefts + rights)
    r1[here] = m1[k]

    @pl.when(jnp.logical_not(owner))
    def _():
        pl.semaphore_wait(known, 1)

    for n, offset in enumerate(chips):
        d = chip_at(offset)
        remote(m1.at[d], r1.at[n], ssem.at[0], rsem.at[0], (2 * d + core, e)).start()
    @pl.when((core == 0) & jnp.logical_not(owner))
    def _():
        lax.fori_loop(split, half, answer, 0)

    for one in loads[3:7]:
        one.wait()
    pack[pl.ds(core, 1)] = jnp.zeros((1, 16, WIDE), F32)
    wide_res = res_v[...].astype(F32)
    pack[core, 0:8, 0:width] = jnp.concatenate([wide_res, wide_res], axis=0)
    pack[core, 8:9, 0:width] = gain_v[...]
    pack[core, 9:10, 0:width] = router_v[...].astype(F32)
    blank = jnp.zeros((2, WIDE - width, wg_v.shape[2]), BF16)
    wg_v[:, width:WIDE, :] = blank
    wu_v[:, width:WIDE, :] = blank
    wd_v[:, width:WIDE, :] = blank
    ids = ids_v[...]
    for x in range(ne):
        hit = jnp.max(jnp.where(ids == x, 1.0, 0.0), axis=1, keepdims=True)
        hit_v[x] = jnp.broadcast_to(hit, (4, WIDE))

    for one in swaps:
        one.start()

    drain(r1.at[pl.ds(0, here)], rsem.at[0])
    peaks, totals = stats_of(r1[:, :, hl:])
    factor = jnp.exp(peaks - jnp.max(peaks, axis=0)[None])
    denom = jnp.sum(factor * totals, axis=0)
    denom = denom[:, 0:1] + denom[:, 64:65]
    columns = []
    for first in (0, 8):
        for a in chunks:
            block = r1[:, :, a : a + WIDE].astype(F32)[:, first : first + 8]
            columns.append(jnp.sum(factor * block, axis=0))
    latent = (jnp.concatenate(columns, axis=1) / denom).astype(BF16)

    loads[7].wait()
    first = jnp.dot(latent, wuv_v[0], preferred_element_type=F32)
    second = jnp.dot(latent, wuv_v[1], preferred_element_type=F32)
    upper = iota((8, WIDE), 0) < 4
    lane = iota((8, WIDE), 1)
    values = jnp.concatenate(
        [
            jnp.where(upper, first, pltpu.roll(first, 4, 0)),
            jnp.where(upper, pltpu.roll(second, 4, 0), second),
        ],
        axis=1,
    ).astype(BF16)
    loads[8].wait()
    group = min(4, nk)
    for g in range(0, nk, group):
        begin, size = 2 * width * g, 2 * width * group
        part = jnp.dot(values, wout_v[:, begin : begin + size], preferred_element_type=F32)
        part = jnp.concatenate([part, jnp.zeros((8, WIDE), F32)], axis=1)
        for i in range(group):
            a = 2 * width * i
            s2[g + i] = jnp.where(upper, part[:, a : a + WIDE], part[:, a + width : a + width + WIDE])

    def send_2(n, d, sem):
        remote(s2.at[d], r2.at[2 * n + core], ssem.at[1], rsem.at[sem], (2 * d + side, e)).start()

    for n, offset in enumerate(chips):
        send_2(n, chip_at(offset), 7 if n < remotes else 1)

    @pl.when(owner)
    def _():
        r2[2 * here + core] = s2[k]

    @pl.when(jnp.logical_not(owner))
    def _():
        send_2(here, k, 1)

    swaps[0].wait_recv()

    @pl.when(owner)
    def _():
        drain(r2.at[pl.ds(0, 2 * (here - remotes) + 1)], rsem.at[1])
        stream = jnp.where(upper, pack[0, 0:8], pack[1, 0:8])
        stream = stream + jnp.sum(r2[2 * remotes :], axis=0)
        if remotes:
            drain(r2.at[pl.ds(0, 2 * remotes)], rsem.at[7])
            stream = stream + jnp.sum(r2[0 : 2 * remotes], axis=0)
        stream = jnp.where(lane < width, stream, 0.0)
        hidden = stream.astype(BF16).astype(F32)
        hid_v[...] = hidden
        st_v[...] = stream
        r3[pl.ds(turn, 1)] = hidden[None]


        @pl.when(place < ne - 1)
        def _():
            pl.semaphore_wait(hello, ne - 1 - place)

        arrived = rsem.at[2 + mine_in]
        for i in far:
            z = (e + i) & (ne - 1)
            remote(hid_v, r3.at[turn], ssem.at[2], arrived, (c, z)).start()
        remote(st_v, st_v, pair_send.at[4], pair_recv.at[4], (partner, e)).start()

    def wait_3(b):
        here_too = owner & (mine_in == b)
        pl.when(here_too)(lambda: drain(r3.at[pl.ds(0, split - 1)], rsem.at[2 + b]))
        pl.when(jnp.logical_not(here_too))(lambda: drain(r3.at[pl.ds(0, split)], rsem.at[2 + b]))

    def send_4(b):
        got = r3[pl.ds(b * split, split)]
        turned = pltpu.roll(got, 4, 1)
        pairs = (split // 2, 2, 8, WIDE)
        top3 = iota((split // 2, 8, WIDE), 1) < 4
        got, turned = got.reshape(pairs), turned.reshape(pairs)
        tokens = [
            jnp.where(top3, got[:, 0], turned[:, 1]).reshape(batch, WIDE),
            jnp.where(top3, turned[:, 0], got[:, 1]).reshape(batch, WIDE),
        ]
        squares = jnp.sum(tokens[0] * tokens[0] + tokens[1] * tokens[1], axis=1, keepdims=True)
        scaled = [(tokens[f] * pack[f, 8:9, :]).astype(BF16) for f in range(2)]
        logits = jnp.sum(
            scaled[0].astype(F32) * pack[0, 9:10, :] + scaled[1].astype(F32) * pack[1, 9:10, :],
            axis=1,
            keepdims=True,
        )
        scaled = jnp.concatenate(scaled, axis=1)
        lane16 = iota((16, WIDE), 1)
        block = jnp.zeros((16, WIDE), F32)
        lane_at = 0
        for stat in (squares, logits):
            for piece in split_two(stat):
                for a in range(0, batch, 16):
                    block = jnp.where(lane16 == lane_at, piece[a : a + 16], block)
                    lane_at += 1
        block = block.astype(BF16)
        gate = jnp.dot(scaled, wg_v[...].reshape(2 * WIDE, -1), preferred_element_type=F32).astype(BF16)
        up = jnp.dot(scaled, wu_v[...].reshape(2 * WIDE, -1), preferred_element_type=F32).astype(BF16)
        for d in range(nk):
            s4[b, d, 0:batch] = gate[:, d * WIDE : (d + 1) * WIDE]
            s4[b, d, batch : 2 * batch] = up[:, d * WIDE : (d + 1) * WIDE]
            s4[b, d, 2 * batch :] = block
        r4[b, here] = s4[b, k]
        for n, offset in enumerate(chips):
            d = chip_at(offset)
            sem = rsem.at[(10 if n < remotes else 8) + b]
            remote(s4.at[b, d], r4.at[b, n], ssem.at[3], sem, (2 * d + core, e)).start()

    def send_5(b):
        drain(r4.at[b, pl.ds(0, here - remotes)], rsem.at[8 + b])
        sums = jnp.sum(r4[b, remotes:].astype(F32), axis=0)
        if remotes:
            drain(r4.at[b, pl.ds(0, remotes)], rsem.at[10 + b])
            sums = sums + jnp.sum(r4[b, 0:remotes].astype(F32), axis=0)
        gate, up, block = sums[0:batch], sums[batch : 2 * batch], sums[2 * batch :]
        parts = batch // 16

        def column(n):
            n = n * parts
            pair = block[:, n : n + parts] + block[:, n + parts : n + 2 * parts]
            return jnp.concatenate([pair[:, a : a + 1] for a in range(parts)], axis=0)

        inverse = lax.rsqrt(column(0) / (width * nc) + EPS)
        score = jax.nn.sigmoid(column(2) * inverse).astype(BF16).astype(F32)
        gate = gate * inverse
        act = gate / (1.0 + jnp.exp(-gate)) * (up * inverse) * score
        act = act.astype(BF16)
        s5[b] = act
        score_v[b] = jnp.broadcast_to(score, (batch, WIDE))
        r5[b, pl.ds(k, 1)] = act[None]
        for offset in chips:
            d = chip_at(offset)
            remote(s5.at[b], r5.at[b, k], ssem.at[4], rsem.at[12 + b], (2 * d + core, e)).start()

    def send_6(b):
        drain(r5.at[b, pl.ds(0, nk - 1)], rsem.at[12 + b])
        act = jnp.concatenate([r5[b, d] for d in range(nk)], axis=1)
        made = lax.dot_general(
            act, wd_v[...].reshape(2 * WIDE, -1), (((1,), (1,)), ((), ())), preferred_element_type=F32
        )
        shown = iota((batch, WIDE), 1) >= width
        for f in range(2):
            block = jnp.where(shown, score_v[b], made[:, f * WIDE : (f + 1) * WIDE])
            s6[f, pl.ds(b * split, split)] = block.reshape(split, 4, WIDE)

        def back(t, f):
            remote(s6.at[f, t], r6.at[e], ssem.at[5], rsem.at[5], (2 * k + f, half * core + t)).start()

        for i in range(1, split + 1):
            t = b * split + ((turn + i) & (split - 1))
            for f in range(2):
                if i == split:
                    pl.when(jnp.logical_not(owner & (core == f) & (mine_in == b)))(functools.partial(back, t, f))
                else:
                    back(t, f)

    first = jnp.where((core == 1) & ((e < split) | (e >= ne - split)), 1, 0)
    second = 1 - first
    wait_3(first)
    for n in (9, 10):
        loads[n].wait()
        swaps[n - 8].wait_recv()
    send_4(first)
    wait_3(second)
    send_4(second)
    send_5(first)
    send_5(second)
    loads[11].wait()
    swaps[3].wait_recv()
    send_6(first)
    send_6(second)

    @pl.when(owner)
    def _():
        r6[pl.ds(e, 1)] = s6[core, pl.ds(turn, 1)]
        drain(r6.at[pl.ds(0, ne - 1)], rsem.at[5])

    @pl.when(jnp.logical_not(owner))
    def _():
        drain(r6, rsem.at[5])
        pltpu.make_async_copy(st_v, st_v, pair_recv.at[4]).wait()

    mixed = jnp.sum(jnp.where(hit_v[...] > 0.0, r6[...], 0.0), axis=0)
    stream = st_v[...]
    stream = jnp.where(core == 1, pltpu.roll(stream, 4, 0), stream)[0:4]
    out_ref[...] = stream[:, 0:width] + ROUTE * mixed[:, 0:width] / mixed[:, width : width + 1]

    swap.wait_send()
    drain(s1.at[pl.ds(0, nk - 1)], ssem.at[0])
    drain(s2.at[pl.ds(0, nk - 1)], ssem.at[1])
    for b in range(2):
        drain(s4.at[b, pl.ds(0, nk - 1)], ssem.at[3])
        drain(r5.at[b, pl.ds(0, nk - 1)], ssem.at[4])
    drain(r6.at[pl.ds(0, ne - 1)], ssem.at[5])

    @pl.when(owner)
    def _():
        for _ in far:
            drain(hid_v, ssem.at[2])
        pltpu.make_async_copy(st_v, st_v, pair_send.at[4]).wait()

    @pl.when(jnp.logical_not(owner))
    def _():
        drain(s2.at[0], ssem.at[1])
        drain(r6.at[0], ssem.at[5])

    for one in swaps:
        one.wait_send()


def per_device(nc, ne, *args):
    (queries, cache, lengths, w_uv, w_out, residual, gain, router, w_gate, w_up, w_down, ids) = args
    nk, half = nc // 2, ne // 2
    width, ff = w_gate.shape[1], w_gate.shape[2]
    split = half // 2
    batch = 4 * split
    hbm = pl.BlockSpec(memory_space=pltpu.HBM)
    vmem = lambda *shape, dtype=F32: pltpu.VMEM(shape, dtype)
    half_type = functools.partial(vmem, dtype=BF16)
    like = lambda x: pltpu.VMEM(x.shape, x.dtype)
    gain = gain.reshape(1, width)
    w_down = jnp.swapaxes(w_down, 1, 2)
    scratch = [
        like(queries), like(cache), pltpu.SMEM(lengths.shape, I32), like(w_uv), like(w_out), like(residual),
        like(gain), like(router),
        half_type(2, WIDE, ff), half_type(2, WIDE, ff), half_type(2, WIDE, ff), like(ids),
        vmem(2, 16, WIDE), vmem(ne, 4, WIDE), vmem(8, WIDE), vmem(8, WIDE),
        half_type(nk, 16, LATENT // 2 + WIDE), half_type(nk, 16, LATENT // 2 + WIDE),
        vmem(nk, 8, LATENT), vmem(nk, 8, WIDE), vmem(nk, 8, WIDE),
        half_type(nk, 16, LATENT // 2 + WIDE), half_type(nk, 16, LATENT // 2 + WIDE),
        vmem(nk, 8, WIDE), vmem(nc, 8, WIDE),
        vmem(half, 8, WIDE),
        half_type(2, nk, 2 * batch + 16, WIDE), half_type(2, nk, 2 * batch + 16, WIDE),
        half_type(2, batch, WIDE), half_type(2, nk, batch, WIDE), vmem(2, batch, WIDE),
        vmem(2, half, 4, WIDE), vmem(ne, 4, WIDE),
        pltpu.SemaphoreType.DMA((12,)),
        pltpu.SemaphoreType.DMA((6,)), pltpu.SemaphoreType.DMA((6,)),
        pltpu.SemaphoreType.DMA((6,)), pltpu.SemaphoreType.DMA((14,)), pltpu.SemaphoreType.REGULAR, pltpu.SemaphoreType.REGULAR,
    ]
    return pl.pallas_call(
        functools.partial(kernel, nc, ne),
        out_shape=jax.ShapeDtypeStruct((4, width), F32),
        in_specs=[hbm] * 12,
        out_specs=pl.BlockSpec(memory_space=pltpu.VMEM),
        scratch_shapes=scratch,
        compiler_params=pltpu.CompilerParams(
            collective_id=0, has_side_effects=True, vmem_limit_bytes=64 * 1024 * 1024
        ),
    )(queries, cache, lengths, w_uv, w_out, residual, gain, router, w_gate, w_up, w_down, ids)


def solution(mesh):
    in_specs = (
        P("ep", None, None),
        P("ep", "ctx", None),
        P("ep"),
        P("ctx", None, None),
        P("ctx", None),
        P("ep", "ctx"),
        P("ctx"),
        P("ep", "ctx"),
        P("ep", "ctx", None),
        P("ep", "ctx", None),
        P("ep", None, "ctx"),
        P("ep", None),
    )
    return jax.shard_map(
        functools.partial(per_device, mesh.shape["ctx"], mesh.shape["ep"]),
        mesh=mesh, in_specs=in_specs, out_specs=P("ep", "ctx"), check_vma=False,
    )
```

```python
import functools

import jax
import jax.numpy as jnp
from jax import lax
from jax.experimental import pallas as pl
from jax.experimental.pallas import tpu as pltpu
from jax.sharding import PartitionSpec as P

SCALE = 192.0 ** (-0.5)
FLOOR = -1e30
EPS = 1e-06
ROUTE = 2.5
LATENT = 512
WIDE = 128
MESH = pl.DeviceIdType.MESH
BF16, F32, I32 = jnp.bfloat16, jnp.float32, jnp.int32


def iota(shape, dim):
    return lax.broadcasted_iota(I32, shape, dim)


def split_two(x):
    high = x.astype(BF16).astype(F32)
    return high, x - high


def kernel(
    nc,
    ne,
    q_h, cache_h, len_h, wuv_h, wout_h, res_h, gain_h, router_h, wg_h, wu_h, wd_h, ids_h,
    out_ref,
    q_v, cache_v, len_s, wuv_v, wout_v, res_v, gain_v, router_v, wg_v, wu_v, wd_v, ids_v,
    pack, hit_v, st_v, hid_v,
    s1, p1, own_v, own_peak, own_total, m1, r1, s2, r2, r3, s4, r4, s5, r5, score_v, s6, r6,
    load_sem, pair_send, pair_recv, ssem, rsem, hello, known,
):
    nk, half = nc // 2, ne // 2
    width = res_h.shape[1]
    span = cache_h.shape[1]
    rows = 8 * nc
    split = half // 2
    batch = 4 * split
    c, e = lax.axis_index("ctx"), lax.axis_index("ep")
    k, core = c >> 1, c & 1
    side = e // half
    turn = e & (half - 1)
    mine_in = turn // split
    owner = core == side
    partner = 2 * k + 1 - core

    def load(n, src, dst):
        return pltpu.make_async_copy(src, dst, load_sem.at[n])

    loads = [
        load(0, q_h, q_v),
        load(1, cache_h, cache_v),
        load(2, len_h, len_s),
        load(3, res_h, res_v),
        load(4, gain_h, gain_v),
        load(5, router_h, router_v),
        load(6, ids_h, ids_v),
        load(7, wuv_h, wuv_v),
        load(8, wout_h, wout_v),
        load(9, wg_h.at[0], wg_v.at[core, pl.ds(0, width)]),
        load(10, wu_h.at[0], wu_v.at[core, pl.ds(0, width)]),
        load(11, wd_h.at[0], wd_v.at[core, pl.ds(0, width)]),
    ]
    for one in loads[:3]:
        one.start()

    place = jnp.where((core == 1) & (e >= half), ne - 1 - (e - half), e)
    base = core * half
    source = (place >= base) & (place < base + half)

    def at_place(p):
        return (c, jnp.where((core == 1) & (p >= half), ne - 1 - (p - half), p))

    xs = 4 if nk % 4 == 0 else nk
    ys = nk // xs
    hops = lambda o: min(o[0], ys - o[0]) + min(o[1], xs - o[1])
    chips = [(dy, dx) for dy in range(ys) for dx in range(xs) if (dy, dx) != (0, 0)]
    chips.sort(key=lambda o: -hops(o))
    remotes = len([o for o in chips if hops(o) > 2])
    here = len(chips)

    peers = {o: ((k // xs + o[0]) & (ys - 1)) * xs + ((k + o[1]) & (xs - 1)) for o in chips}

    def chip_at(offset):
        return peers[offset]

    barrier = pltpu.get_barrier_semaphore()

    def greet(to):
        pl.semaphore_signal(barrier, inc=1, device_id=to, device_id_type=MESH)

    for offset in chips:
        greet((2 * chip_at(offset) + side, e))

    @pl.when(owner)
    def _():
        greet((partner, e))

    def greet_ep(p, _):
        z = at_place(p)[1]
        greet((2 * k + jnp.where((core == 0) & (place < split), 0, z // half), z))
        return 0

    first_up = jnp.where(core == 0, jnp.where(source, place + 1, ne), jnp.maximum(place + 1, half))
    lax.fori_loop(first_up, ne, greet_ep, 0)
    greeted = jnp.where(
        owner,
        2 * (nk - 1) + place + jnp.where(core == 1, half - split, 0),
        1 + jnp.where(core == 0, split, 0),
    )

    def answer(p, _):
        pl.semaphore_signal(hello, inc=1, device_id=at_place(p), device_id_type=MESH)
        return 0

    far = sorted(range(1, ne), key=lambda i: -min(i, ne - i))

    def remote(src, dst, send, recv, to):
        return pltpu.make_async_remote_copy(
            src_ref=src, dst_ref=dst, send_sem=send, recv_sem=recv, device_id=to, device_id_type=MESH
        )

    def drain(ref, sem):
        pltpu.make_async_copy(ref, ref, sem).wait()

    for one in loads[3:7]:
        one.start()

    def tell_partner():
        pl.semaphore_signal(known, inc=1, device_id=(partner, e), device_id_type=MESH)

    loads[0].wait()
    row = iota((rows, rows), 0)
    other = row >= 8 * nk
    want = (row & 3) * (2 * nc) + 4 * ((row >> 3) - jnp.where(other, nk, 0)) + ((row >> 2) & 1)
    want = want + 2 * jnp.where(other, 1 - core, core)
    order = jnp.where(iota((rows, rows), 1) == want, 1.0, 0.0).astype(BF16)
    q = q_v[...].reshape(rows, q_v.shape[2])
    q = jnp.dot(order, q, preferred_element_type=F32).astype(BF16)
    loads[1].wait()
    for one in loads[7:]:
        one.start()
    loads[2].wait()
    keys = cache_v[...].reshape(4 * span, cache_v.shape[2])
    scores = lax.dot_general(q, keys, (((1,), (1,)), ((), ())), preferred_element_type=F32) * SCALE
    col = iota((1, 4 * span), 1)
    col_row = jnp.zeros_like(col)
    limit = jnp.full_like(col, len_s[0])
    for r in range(1, 4):
        past = col >= r * span
        col_row = jnp.where(past, r, col_row)
        limit = jnp.where(past, len_s[r], limit)
    position = c * span + col - col_row * span
    col_row = jnp.where(position < limit, col_row, -1)
    valid = (iota((rows, 4 * span), 0) & 3) == col_row
    masked = jnp.where(valid, scores, FLOOR)
    peak = jnp.max(masked, axis=1, keepdims=True).astype(BF16).astype(F32)

    @pl.when(jnp.logical_not(owner))
    def _():
        pl.semaphore_wait(barrier, greeted)
        tell_partner()

        @pl.when(core == 0)
        def _():
            lax.fori_loop(0, split, answer, 0)

    weights = jnp.where(valid, jnp.exp(masked - peak), 0.0).astype(BF16)
    total = jnp.sum(weights.astype(F32), axis=1, keepdims=True)
    summed = jnp.dot(weights, keys[:, :LATENT], preferred_element_type=F32)
    summed = summed.reshape(2, nk, 8, LATENT)
    hl = LATENT // 2
    chunks = range(0, hl, WIDE)
    peaks = jnp.broadcast_to(peak, (rows, WIDE)).reshape(2, nk, 8, WIDE)
    totals = jnp.broadcast_to(total, (rows, WIDE)).reshape(2, nk, 8, WIDE)
    side_lane = iota((nk, 8, WIDE), 2) < 64

    def put(ref, top, amount, parts):
        high, rest = split_two(amount)
        for n, a in enumerate(chunks):
            ref[:, :, a : a + WIDE] = jnp.concatenate([parts[n], parts[n + len(chunks)]], axis=1).astype(BF16)
        ref[:, :, hl:] = jnp.concatenate([top, jnp.where(side_lane, high, rest)], axis=1).astype(BF16)

    columns = range(0, LATENT, WIDE)
    put(s1, peaks[1], totals[1], [summed[1, :, :, a : a + WIDE] for a in columns])
    own_v[...] = summed[0]
    own_peak[...] = peaks[0]
    own_total[...] = totals[0]

    swap = remote(s1, p1, pair_send.at[5], pair_recv.at[5], (partner, e))

    @pl.when(owner)
    def _():
        pl.semaphore_wait(known, 1)
        swap.start()
        pl.semaphore_wait(barrier, greeted)
        tell_partner()
        lax.fori_loop(base, place, answer, 0)

    pl.when(jnp.logical_not(owner))(swap.start)

    mine = pl.ds(0, width)
    swaps = [
        remote(pack.at[core], pack.at[core], pair_send.at[0], pair_recv.at[0], (partner, e)),
        remote(wg_h.at[0], wg_v.at[core, mine], pair_send.at[1], pair_recv.at[1], (partner, e)),
        remote(wu_h.at[0], wu_v.at[core, mine], pair_send.at[2], pair_recv.at[2], (partner, e)),
        remote(wd_h.at[0], wd_v.at[core, mine], pair_send.at[3], pair_recv.at[3], (partner, e)),
    ]
    swap.wait_recv()

    def stats_of(x):
        x = x.astype(F32)
        return x[:, 0:8], x[:, 8:16]

    peaks, totals = stats_of(p1[:, :, hl:])
    totals = totals + pltpu.roll(totals, 64, 2)
    top = jnp.maximum(peaks, own_peak[...])
    from_own, from_other = jnp.exp(own_peak[...] - top), jnp.exp(peaks - top)
    lefts, rights = [], []
    for a in chunks:
        block = p1[:, :, a : a + WIDE].astype(F32)
        lefts.append(from_own * own_v[:, :, a : a + WIDE] + from_other * block[:, 0:8])
        rights.append(from_own * own_v[:, :, hl + a : hl + a + WIDE] + from_other * block[:, 8:16])
    put(m1, top, from_own * own_total[...] + from_other * totals, lefts + rights)
    r1[here] = m1[k]

    @pl.when(jnp.logical_not(owner))
    def _():
        pl.semaphore_wait(known, 1)

    for n, offset in enumerate(chips):
        d = chip_at(offset)
        remote(m1.at[d], r1.at[n], ssem.at[0], rsem.at[0], (2 * d + core, e)).start()
    @pl.when((core == 0) & jnp.logical_not(owner))
    def _():
        lax.fori_loop(split, half, answer, 0)

    for one in loads[3:7]:
        one.wait()
    pack[pl.ds(core, 1)] = jnp.zeros((1, 16, WIDE), F32)
    wide_res = res_v[...].astype(F32)
    pack[core, 0:8, 0:width] = jnp.concatenate([wide_res, wide_res], axis=0)
    pack[core, 8:9, 0:width] = gain_v[...]
    pack[core, 9:10, 0:width] = router_v[...].astype(F32)
    blank = jnp.zeros((2, WIDE - width, wg_v.shape[2]), BF16)
    wg_v[:, width:WIDE, :] = blank
    wu_v[:, width:WIDE, :] = blank
    wd_v[:, width:WIDE, :] = blank
    ids = ids_v[...]
    for x in range(ne):
        hit = jnp.max(jnp.where(ids == x, 1.0, 0.0), axis=1, keepdims=True)
        hit_v[x] = jnp.broadcast_to(hit, (4, WIDE))

    for one in swaps:
        one.start()

    drain(r1.at[pl.ds(0, here)], rsem.at[0])
    peaks, totals = stats_of(r1[:, :, hl:])
    factor = jnp.exp(peaks - jnp.max(peaks, axis=0)[None])
    denom = jnp.sum(factor * totals, axis=0)
    denom = denom[:, 0:1] + denom[:, 64:65]
    columns = []
    for first in (0, 8):
        for a in chunks:
            block = r1[:, :, a : a + WIDE].astype(F32)[:, first : first + 8]
            columns.append(jnp.sum(factor * block, axis=0))
    latent = (jnp.concatenate(columns, axis=1) / denom).astype(BF16)

    loads[7].wait()
    first = jnp.dot(latent, wuv_v[0], preferred_element_type=F32)
    second = jnp.dot(latent, wuv_v[1], preferred_element_type=F32)
    upper = iota((8, WIDE), 0) < 4
    lane = iota((8, WIDE), 1)
    values = jnp.concatenate(
        [
            jnp.where(upper, first, pltpu.roll(first, 4, 0)),
            jnp.where(upper, pltpu.roll(second, 4, 0), second),
        ],
        axis=1,
    ).astype(BF16)
    loads[8].wait()
    group = min(4, nk)
    for g in range(0, nk, group):
        begin, size = 2 * width * g, 2 * width * group
        part = jnp.dot(values, wout_v[:, begin : begin + size], preferred_element_type=F32)
        part = jnp.concatenate([part, jnp.zeros((8, WIDE), F32)], axis=1)
        for i in range(group):
            a = 2 * width * i
            s2[g + i] = jnp.where(upper, part[:, a : a + WIDE], part[:, a + width : a + width + WIDE])

    def send_2(n, d, sem):
        remote(s2.at[d], r2.at[2 * n + core], ssem.at[1], rsem.at[sem], (2 * d + side, e)).start()

    for n, offset in enumerate(chips):
        send_2(n, chip_at(offset), 7 if n < remotes else 1)

    @pl.when(owner)
    def _():
        r2[2 * here + core] = s2[k]

    @pl.when(jnp.logical_not(owner))
    def _():
        send_2(here, k, 1)

    swaps[0].wait_recv()

    @pl.when(owner)
    def _():
        drain(r2.at[pl.ds(0, 2 * (here - remotes) + 1)], rsem.at[1])
        stream = jnp.where(upper, pack[0, 0:8], pack[1, 0:8])
        stream = stream + jnp.sum(r2[2 * remotes :], axis=0)
        if remotes:
            drain(r2.at[pl.ds(0, 2 * remotes)], rsem.at[7])
            stream = stream + jnp.sum(r2[0 : 2 * remotes], axis=0)
        stream = jnp.where(lane < width, stream, 0.0)
        hidden = stream.astype(BF16).astype(F32)
        hid_v[...] = hidden
        st_v[...] = stream
        r3[pl.ds(turn, 1)] = hidden[None]


        @pl.when(place < ne - 1)
        def _():
            pl.semaphore_wait(hello, ne - 1 - place)

        arrived = rsem.at[2 + mine_in]
        for i in far:
            z = (e + i) & (ne - 1)
            remote(hid_v, r3.at[turn], ssem.at[2], arrived, (c, z)).start()
        remote(st_v, st_v, pair_send.at[4], pair_recv.at[4], (partner, e)).start()

    def wait_3(b):
        here_too = owner & (mine_in == b)
        pl.when(here_too)(lambda: drain(r3.at[pl.ds(0, split - 1)], rsem.at[2 + b]))
        pl.when(jnp.logical_not(here_too))(lambda: drain(r3.at[pl.ds(0, split)], rsem.at[2 + b]))

    def send_4(b):
        got = r3[pl.ds(b * split, split)]
        turned = pltpu.roll(got, 4, 1)
        pairs = (split // 2, 2, 8, WIDE)
        top3 = iota((split // 2, 8, WIDE), 1) < 4
        got, turned = got.reshape(pairs), turned.reshape(pairs)
        tokens = [
            jnp.where(top3, got[:, 0], turned[:, 1]).reshape(batch, WIDE),
            jnp.where(top3, turned[:, 0], got[:, 1]).reshape(batch, WIDE),
        ]
        squares = jnp.sum(tokens[0] * tokens[0] + tokens[1] * tokens[1], axis=1, keepdims=True)
        scaled = [(tokens[f] * pack[f, 8:9, :]).astype(BF16) for f in range(2)]
        logits = jnp.sum(
            scaled[0].astype(F32) * pack[0, 9:10, :] + scaled[1].astype(F32) * pack[1, 9:10, :],
            axis=1,
            keepdims=True,
        )
        scaled = jnp.concatenate(scaled, axis=1)
        lane16 = iota((16, WIDE), 1)
        block = jnp.zeros((16, WIDE), F32)
        lane_at = 0
        for stat in (squares, logits):
            for piece in split_two(stat):
                for a in range(0, batch, 16):
                    block = jnp.where(lane16 == lane_at, piece[a : a + 16], block)
                    lane_at += 1
        block = block.astype(BF16)
        gate = jnp.dot(scaled, wg_v[...].reshape(2 * WIDE, -1), preferred_element_type=F32).astype(BF16)
        up = jnp.dot(scaled, wu_v[...].reshape(2 * WIDE, -1), preferred_element_type=F32).astype(BF16)
        for d in range(nk):
            s4[b, d, 0:batch] = gate[:, d * WIDE : (d + 1) * WIDE]
            s4[b, d, batch : 2 * batch] = up[:, d * WIDE : (d + 1) * WIDE]
            s4[b, d, 2 * batch :] = block
        r4[b, here] = s4[b, k]
        for n, offset in enumerate(chips):
            d = chip_at(offset)
            sem = rsem.at[(10 if n < remotes else 8) + b]
            remote(s4.at[b, d], r4.at[b, n], ssem.at[3], sem, (2 * d + core, e)).start()

    def send_5(b):
        drain(r4.at[b, pl.ds(0, here - remotes)], rsem.at[8 + b])
        sums = jnp.sum(r4[b, remotes:].astype(F32), axis=0)
        if remotes:
            drain(r4.at[b, pl.ds(0, remotes)], rsem.at[10 + b])
            sums = sums + jnp.sum(r4[b, 0:remotes].astype(F32), axis=0)
        gate, up, block = sums[0:batch], sums[batch : 2 * batch], sums[2 * batch :]
        parts = batch // 16

        def column(n):
            n = n * parts
            pair = block[:, n : n + parts] + block[:, n + parts : n + 2 * parts]
            return jnp.concatenate([pair[:, a : a + 1] for a in range(parts)], axis=0)

        inverse = lax.rsqrt(column(0) / (width * nc) + EPS)
        score = jax.nn.sigmoid(column(2) * inverse).astype(BF16).astype(F32)
        gate = gate * inverse
        act = gate / (1.0 + jnp.exp(-gate)) * (up * inverse) * score
        act = act.astype(BF16)
        s5[b] = act
        score_v[b] = jnp.broadcast_to(score, (batch, WIDE))
        r5[b, pl.ds(k, 1)] = act[None]
        for offset in chips:
            d = chip_at(offset)
            remote(s5.at[b], r5.at[b, k], ssem.at[4], rsem.at[12 + b], (2 * d + core, e)).start()

    def send_6(b):
        drain(r5.at[b, pl.ds(0, nk - 1)], rsem.at[12 + b])
        act = jnp.concatenate([r5[b, d] for d in range(nk)], axis=1)
        made = lax.dot_general(
            act, wd_v[...].reshape(2 * WIDE, -1), (((1,), (1,)), ((), ())), preferred_element_type=F32
        )
        shown = iota((batch, WIDE), 1) >= width
        for f in range(2):
            block = jnp.where(shown, score_v[b], made[:, f * WIDE : (f + 1) * WIDE])
            s6[f, pl.ds(b * split, split)] = block.reshape(split, 4, WIDE)

        def back(t, f):
            remote(s6.at[f, t], r6.at[e], ssem.at[5], rsem.at[5], (2 * k + f, half * core + t)).start()

        for i in range(1, split + 1):
            t = b * split + ((turn + i) & (split - 1))
            for f in range(2):
                if i == split:
                    pl.when(jnp.logical_not(owner & (core == f) & (mine_in == b)))(functools.partial(back, t, f))
                else:
                    back(t, f)

    first = jnp.where((core == 1) & ((e < split) | (e >= ne - split)), 1, 0)
    second = 1 - first
    wait_3(first)
    for n in (9, 10):
        loads[n].wait()
        swaps[n - 8].wait_recv()
    send_4(first)
    wait_3(second)
    send_4(second)
    send_5(first)
    send_5(second)
    loads[11].wait()
    swaps[3].wait_recv()
    send_6(first)
    send_6(second)

    @pl.when(owner)
    def _():
        r6[pl.ds(e, 1)] = s6[core, pl.ds(turn, 1)]
        drain(r6.at[pl.ds(0, ne - 1)], rsem.at[5])

    @pl.when(jnp.logical_not(owner))
    def _():
        drain(r6, rsem.at[5])
        pltpu.make_async_copy(st_v, st_v, pair_recv.at[4]).wait()

    mixed = jnp.sum(jnp.where(hit_v[...] > 0.0, r6[...], 0.0), axis=0)
    stream = st_v[...]
    stream = jnp.where(core == 1, pltpu.roll(stream, 4, 0), stream)[0:4]
    out_ref[...] = stream[:, 0:width] + ROUTE * mixed[:, 0:width] / mixed[:, width : width + 1]

    swap.wait_send()
    drain(s1.at[pl.ds(0, nk - 1)], ssem.at[0])
    drain(s2.at[pl.ds(0, nk - 1)], ssem.at[1])
    for b in range(2):
        drain(s4.at[b, pl.ds(0, nk - 1)], ssem.at[3])
        drain(r5.at[b, pl.ds(0, nk - 1)], ssem.at[4])
    drain(r6.at[pl.ds(0, ne - 1)], ssem.at[5])

    @pl.when(owner)
    def _():
        for _ in far:
            drain(hid_v, ssem.at[2])
        pltpu.make_async_copy(st_v, st_v, pair_send.at[4]).wait()

    @pl.when(jnp.logical_not(owner))
    def _():
        drain(s2.at[0], ssem.at[1])
        drain(r6.at[0], ssem.at[5])

    for one in swaps:
        one.wait_send()


def per_device(nc, ne, *args):
    (queries, cache, lengths, w_uv, w_out, residual, gain, router, w_gate, w_up, w_down, ids) = args
    nk, half = nc // 2, ne // 2
    width, ff = w_gate.shape[1], w_gate.shape[2]
    split = half // 2
    batch = 4 * split
    hbm = pl.BlockSpec(memory_space=pltpu.HBM)
    vmem = lambda *shape, dtype=F32: pltpu.VMEM(shape, dtype)
    half_type = functools.partial(vmem, dtype=BF16)
    like = lambda x: pltpu.VMEM(x.shape, x.dtype)
    gain = gain.reshape(1, width)
    w_down = jnp.swapaxes(w_down, 1, 2)
    scratch = [
        like(queries), like(cache), pltpu.SMEM(lengths.shape, I32), like(w_uv), like(w_out), like(residual),
        like(gain), like(router),
        half_type(2, WIDE, ff), half_type(2, WIDE, ff), half_type(2, WIDE, ff), like(ids),
        vmem(2, 16, WIDE), vmem(ne, 4, WIDE), vmem(8, WIDE), vmem(8, WIDE),
        half_type(nk, 16, LATENT // 2 + WIDE), half_type(nk, 16, LATENT // 2 + WIDE),
        vmem(nk, 8, LATENT), vmem(nk, 8, WIDE), vmem(nk, 8, WIDE),
        half_type(nk, 16, LATENT // 2 + WIDE), half_type(nk, 16, LATENT // 2 + WIDE),
        vmem(nk, 8, WIDE), vmem(nc, 8, WIDE),
        vmem(half, 8, WIDE),
        half_type(2, nk, 2 * batch + 16, WIDE), half_type(2, nk, 2 * batch + 16, WIDE),
        half_type(2, batch, WIDE), half_type(2, nk, batch, WIDE), vmem(2, batch, WIDE),
        vmem(2, half, 4, WIDE), vmem(ne, 4, WIDE),
        pltpu.SemaphoreType.DMA((12,)),
        pltpu.SemaphoreType.DMA((6,)), pltpu.SemaphoreType.DMA((6,)),
        pltpu.SemaphoreType.DMA((6,)), pltpu.SemaphoreType.DMA((14,)), pltpu.SemaphoreType.REGULAR, pltpu.SemaphoreType.REGULAR,
    ]
    return pl.pallas_call(
        functools.partial(kernel, nc, ne),
        out_shape=pltpu.VMEM((4, width), F32),
        in_specs=[hbm] * 12,
        out_specs=pl.BlockSpec(memory_space=pltpu.VMEM),
        scratch_shapes=scratch,
        compiler_params=pltpu.CompilerParams(
            collective_id=0, has_side_effects=True, vmem_limit_bytes=60 * 1024 * 1024
        ),
    )(queries, cache, lengths, w_uv, w_out, residual, gain, router, w_gate, w_up, w_down, ids)


def solution(mesh):
    in_specs = (
        P("ep", None, None),
        P("ep", "ctx", None),
        P("ep"),
        P("ctx", None, None),
        P("ctx", None),
        P("ep", "ctx"),
        P("ctx"),
        P("ep", "ctx"),
        P("ep", "ctx", None),
        P("ep", "ctx", None),
        P("ep", None, "ctx"),
        P("ep", None),
    )
    return jax.shard_map(
        functools.partial(per_device, mesh.shape["ctx"], mesh.shape["ep"]),
        mesh=mesh, in_specs=in_specs, out_specs=P("ep", "ctx"), check_vma=False,
    )
```

```python
import functools

import jax
import jax.numpy as jnp
from jax import lax
from jax.experimental import pallas as pl
from jax.experimental.pallas import tpu as pltpu
from jax.sharding import PartitionSpec as P

SCALE = 192.0 ** (-0.5)
FLOOR = -1e30
EPS = 1e-06
ROUTE = 2.5
LATENT = 512
WIDE = 128
MESH = pl.DeviceIdType.MESH
BF16, F32, I32 = jnp.bfloat16, jnp.float32, jnp.int32


def iota(shape, dim):
    return lax.broadcasted_iota(I32, shape, dim)


def split_two(x):
    high = x.astype(BF16).astype(F32)
    return high, x - high


def kernel(
    nc,
    ne,
    q_h, cache_h, len_h, wuv_h, wout_h, res_h, gain_h, router_h, wg_h, wu_h, wd_h, ids_h,
    out_ref,
    q_v, cache_v, len_s, wuv_v, wout_v, res_v, gain_v, router_v, wg_v, wu_v, wd_v, ids_v,
    pack, hit_v, st_v, hid_v,
    s1, p1, own_v, own_peak, own_total, m1, r1, m7, r8, s2, r2, r3, s4, r4, s7, r7, s5, r5, score_v, s6, r6,
    load_sem, pair_send, pair_recv, ssem, rsem, hello, known,
):
    nk, half = nc // 2, ne // 2
    width = res_h.shape[1]
    span = cache_h.shape[1]
    rows = 8 * nc
    split = half // 2
    batch = 4 * split
    c, e = lax.axis_index("ctx"), lax.axis_index("ep")
    k, core = c >> 1, c & 1
    side = e // half
    turn = e & (half - 1)
    mine_in = turn // split
    owner = core == side
    partner = 2 * k + 1 - core

    def load(n, src, dst):
        return pltpu.make_async_copy(src, dst, load_sem.at[n])

    loads = [
        load(0, q_h, q_v),
        load(1, cache_h, cache_v),
        load(2, len_h, len_s),
        load(3, res_h, res_v),
        load(4, gain_h, gain_v),
        load(5, router_h, router_v),
        load(6, ids_h, ids_v),
        load(7, wuv_h, wuv_v),
        load(8, wout_h, wout_v),
        load(9, wg_h.at[0], wg_v.at[core, pl.ds(0, width)]),
        load(10, wu_h.at[0], wu_v.at[core, pl.ds(0, width)]),
        load(11, wd_h.at[0], wd_v.at[core, pl.ds(0, width)]),
    ]
    for one in loads[:3]:
        one.start()

    place = jnp.where((core == 1) & (e >= half), ne - 1 - (e - half), e)
    base = core * half
    source = (place >= base) & (place < base + half)

    def at_place(p):
        return (c, jnp.where((core == 1) & (p >= half), ne - 1 - (p - half), p))

    xs = 4 if nk % 4 == 0 else nk
    ys = nk // xs
    hops = lambda o: min(o[0], ys - o[0]) + min(o[1], xs - o[1])
    chips = [(dy, dx) for dy in range(ys) for dx in range(xs) if (dy, dx) != (0, 0)]
    chips.sort(key=lambda o: -hops(o))
    remotes = len([o for o in chips if hops(o) > 2])
    here = len(chips)

    peers = {o: ((k // xs + o[0]) & (ys - 1)) * xs + ((k + o[1]) & (xs - 1)) for o in chips}

    def chip_at(offset):
        return peers[offset]

    barrier = pltpu.get_barrier_semaphore()

    def greet(to):
        pl.semaphore_signal(barrier, inc=1, device_id=to, device_id_type=MESH)

    for offset in chips:
        greet((2 * chip_at(offset) + side, e))

    @pl.when(owner)
    def _():
        greet((partner, e))

    def greet_ep(p, _):
        z = at_place(p)[1]
        greet((2 * k + jnp.where((core == 0) & (place < split), 0, z // half), z))
        return 0

    first_up = jnp.where(core == 0, jnp.where(source, place + 1, ne), jnp.maximum(place + 1, half))
    lax.fori_loop(first_up, ne, greet_ep, 0)
    greeted = jnp.where(
        owner,
        2 * (nk - 1) + place + jnp.where(core == 1, half - split, 0),
        1 + jnp.where(core == 0, split, 0),
    )

    def answer(p, _):
        pl.semaphore_signal(hello, inc=1, device_id=at_place(p), device_id_type=MESH)
        return 0

    far = sorted(range(1, ne), key=lambda i: -min(i, ne - i))

    def remote(src, dst, send, recv, to):
        return pltpu.make_async_remote_copy(
            src_ref=src, dst_ref=dst, send_sem=send, recv_sem=recv, device_id=to, device_id_type=MESH
        )

    def drain(ref, sem):
        pltpu.make_async_copy(ref, ref, sem).wait()

    for one in loads[3:7]:
        one.start()

    def tell_partner():
        pl.semaphore_signal(known, inc=1, device_id=(partner, e), device_id_type=MESH)

    loads[0].wait()
    row = iota((rows, rows), 0)
    other = row >= 8 * nk
    want = (row & 3) * (2 * nc) + 4 * ((row >> 3) - jnp.where(other, nk, 0)) + ((row >> 2) & 1)
    want = want + 2 * jnp.where(other, 1 - core, core)
    order = jnp.where(iota((rows, rows), 1) == want, 1.0, 0.0).astype(BF16)
    q = q_v[...].reshape(rows, q_v.shape[2])
    q = jnp.dot(order, q, preferred_element_type=F32).astype(BF16)
    loads[1].wait()
    for one in loads[7:]:
        one.start()
    loads[2].wait()
    keys = cache_v[...].reshape(4 * span, cache_v.shape[2])
    scores = lax.dot_general(q, keys, (((1,), (1,)), ((), ())), preferred_element_type=F32) * SCALE
    col = iota((1, 4 * span), 1)
    col_row = jnp.zeros_like(col)
    limit = jnp.full_like(col, len_s[0])
    for r in range(1, 4):
        past = col >= r * span
        col_row = jnp.where(past, r, col_row)
        limit = jnp.where(past, len_s[r], limit)
    position = c * span + col - col_row * span
    col_row = jnp.where(position < limit, col_row, -1)
    valid = (iota((rows, 4 * span), 0) & 3) == col_row
    masked = jnp.where(valid, scores, FLOOR)
    peak = jnp.max(masked, axis=1, keepdims=True).astype(BF16).astype(F32)

    @pl.when(jnp.logical_not(owner))
    def _():
        pl.semaphore_wait(barrier, greeted)
        tell_partner()

        @pl.when(core == 0)
        def _():
            lax.fori_loop(0, split, answer, 0)

    weights = jnp.where(valid, jnp.exp(masked - peak), 0.0).astype(BF16)
    total = jnp.sum(weights.astype(F32), axis=1, keepdims=True)
    summed = jnp.dot(weights, keys[:, :LATENT], preferred_element_type=F32)
    summed = summed.reshape(2, nk, 8, LATENT)
    hl = LATENT // 2
    chunks = range(0, hl, WIDE)
    peaks = jnp.broadcast_to(peak, (rows, WIDE)).reshape(2, nk, 8, WIDE)
    totals = jnp.broadcast_to(total, (rows, WIDE)).reshape(2, nk, 8, WIDE)
    side_lane = iota((nk, 8, WIDE), 2) < 64

    def put(ref, top, amount, parts):
        high, rest = split_two(amount)
        for n, a in enumerate(chunks):
            ref[:, :, a : a + WIDE] = jnp.concatenate([parts[n], parts[n + len(chunks)]], axis=1).astype(BF16)
        ref[:, :, hl:] = jnp.concatenate([top, jnp.where(side_lane, high, rest)], axis=1).astype(BF16)

    columns = range(0, LATENT, WIDE)
    put(s1, peaks[1], totals[1], [summed[1, :, :, a : a + WIDE] for a in columns])
    own_v[...] = summed[0]
    own_peak[...] = peaks[0]
    own_total[...] = totals[0]

    swap = remote(s1, p1, pair_send.at[5], pair_recv.at[5], (partner, e))

    @pl.when(owner)
    def _():
        pl.semaphore_wait(known, 1)
        swap.start()
        pl.semaphore_wait(barrier, greeted)
        tell_partner()
        lax.fori_loop(base, place, answer, 0)

    pl.when(jnp.logical_not(owner))(swap.start)

    mine = pl.ds(0, width)
    swaps = [
        remote(pack.at[core], pack.at[core], pair_send.at[0], pair_recv.at[0], (partner, e)),
        remote(wg_h.at[0], wg_v.at[core, mine], pair_send.at[1], pair_recv.at[1], (partner, e)),
        remote(wu_h.at[0], wu_v.at[core, mine], pair_send.at[2], pair_recv.at[2], (partner, e)),
        remote(wd_h.at[0], wd_v.at[core, mine], pair_send.at[3], pair_recv.at[3], (partner, e)),
    ]
    swap.wait_recv()

    def stats_of(x):
        x = x.astype(F32)
        return x[:, 0:8], x[:, 8:16]

    peaks, totals = stats_of(p1[:, :, hl:])
    totals = totals + pltpu.roll(totals, 64, 2)
    top = jnp.maximum(peaks, own_peak[...])
    from_own, from_other = jnp.exp(own_peak[...] - top), jnp.exp(peaks - top)
    lefts, rights = [], []
    for a in chunks:
        block = p1[:, :, a : a + WIDE].astype(F32)
        lefts.append(from_own * own_v[:, :, a : a + WIDE] + from_other * block[:, 0:8])
        rights.append(from_own * own_v[:, :, hl + a : hl + a + WIDE] + from_other * block[:, 8:16])
    for n, a in enumerate(chunks):
        m1[:, :, a : a + WIDE] = jnp.concatenate([lefts[n], rights[n]], axis=1).astype(BF16)
    eight = iota((nk, 8, WIDE), 1) == iota((nk, 8, WIDE), 2)
    for n, stat in enumerate((top, from_own * own_total[...] + from_other * totals)):
        m7[:, n : n + 1] = jnp.sum(jnp.where(eight, stat, 0.0), axis=1, keepdims=True)
    r1[here] = m1[k]
    r8[here] = m7[k]

    @pl.when(jnp.logical_not(owner))
    def _():
        pl.semaphore_wait(known, 1)

    for group in (chips[:remotes], chips[remotes:]):
        begin = chips.index(group[0]) if group else 0
        for n, offset in enumerate(group, begin):
            d = chip_at(offset)
            remote(m1.at[d], r1.at[n], ssem.at[0], rsem.at[0], (2 * d + core, e)).start()
        for n, offset in enumerate(group, begin):
            d = chip_at(offset)
            remote(m7.at[d], r8.at[n], ssem.at[7], rsem.at[16], (2 * d + core, e)).start()
    @pl.when((core == 0) & jnp.logical_not(owner))
    def _():
        lax.fori_loop(split, half, answer, 0)

    for one in loads[3:7]:
        one.wait()
    pack[pl.ds(core, 1)] = jnp.zeros((1, 16, WIDE), F32)
    wide_res = res_v[...].astype(F32)
    pack[core, 0:8, 0:width] = jnp.concatenate([wide_res, wide_res], axis=0)
    pack[core, 8:9, 0:width] = gain_v[...]
    pack[core, 9:10, 0:width] = router_v[...].astype(F32)
    blank = jnp.zeros((2, WIDE - width, wg_v.shape[2]), BF16)
    wg_v[:, width:WIDE, :] = blank
    wu_v[:, width:WIDE, :] = blank
    wd_v[:, width:WIDE, :] = blank
    ids = ids_v[...]
    for x in range(ne):
        hit = jnp.max(jnp.where(ids == x, 1.0, 0.0), axis=1, keepdims=True)
        hit_v[x] = jnp.broadcast_to(hit, (4, WIDE))

    for one in swaps:
        one.start()

    drain(r1.at[pl.ds(0, here)], rsem.at[0])
    drain(r8.at[pl.ds(0, here)], rsem.at[16])
    peaks, totals = (
        jnp.sum(jnp.where(eight, r8[:, n : n + 1], 0.0), axis=2, keepdims=True) for n in range(2)
    )
    factor = jnp.exp(peaks - jnp.max(peaks, axis=0)[None])
    denom = jnp.sum(factor * totals, axis=0)
    factor = jnp.broadcast_to(factor, (nk, 8, WIDE))
    columns = []
    for first in (0, 8):
        for a in chunks:
            block = r1[:, :, a : a + WIDE].astype(F32)[:, first : first + 8]
            columns.append(jnp.sum(factor * block, axis=0))
    latent = (jnp.concatenate(columns, axis=1) / denom).astype(BF16)

    loads[7].wait()
    first = jnp.dot(latent, wuv_v[0], preferred_element_type=F32)
    second = jnp.dot(latent, wuv_v[1], preferred_element_type=F32)
    upper = iota((8, WIDE), 0) < 4
    lane = iota((8, WIDE), 1)
    values = jnp.concatenate(
        [
            jnp.where(upper, first, pltpu.roll(first, 4, 0)),
            jnp.where(upper, pltpu.roll(second, 4, 0), second),
        ],
        axis=1,
    ).astype(BF16)
    loads[8].wait()
    group = min(4, nk)
    for g in range(0, nk, group):
        begin, size = 2 * width * g, 2 * width * group
        part = jnp.dot(values, wout_v[:, begin : begin + size], preferred_element_type=F32)
        part = jnp.concatenate([part, jnp.zeros((8, WIDE), F32)], axis=1)
        for i in range(group):
            a = 2 * width * i
            s2[g + i] = jnp.where(upper, part[:, a : a + WIDE], part[:, a + width : a + width + WIDE])

    def send_2(n, d, sem):
        remote(s2.at[d], r2.at[2 * n + core], ssem.at[1], rsem.at[sem], (2 * d + side, e)).start()

    for n, offset in enumerate(chips):
        send_2(n, chip_at(offset), 7 if n < remotes else 1)

    @pl.when(owner)
    def _():
        r2[2 * here + core] = s2[k]

    @pl.when(jnp.logical_not(owner))
    def _():
        send_2(here, k, 1)

    swaps[0].wait_recv()

    @pl.when(owner)
    def _():
        drain(r2.at[pl.ds(0, 2 * (here - remotes) + 1)], rsem.at[1])
        stream = jnp.where(upper, pack[0, 0:8], pack[1, 0:8])
        stream = stream + jnp.sum(r2[2 * remotes :], axis=0)
        if remotes:
            drain(r2.at[pl.ds(0, 2 * remotes)], rsem.at[7])
            stream = stream + jnp.sum(r2[0 : 2 * remotes], axis=0)
        stream = jnp.where(lane < width, stream, 0.0)
        hidden = stream.astype(BF16).astype(F32)
        hid_v[...] = hidden
        st_v[...] = stream
        r3[pl.ds(turn, 1)] = hidden[None]


        @pl.when(place < ne - 1)
        def _():
            pl.semaphore_wait(hello, ne - 1 - place)

        arrived = rsem.at[2 + mine_in]
        for i in far:
            z = (e + i) & (ne - 1)
            remote(hid_v, r3.at[turn], ssem.at[2], arrived, (c, z)).start()
        remote(st_v, st_v, pair_send.at[4], pair_recv.at[4], (partner, e)).start()

    def wait_3(b):
        here_too = owner & (mine_in == b)
        pl.when(here_too)(lambda: drain(r3.at[pl.ds(0, split - 1)], rsem.at[2 + b]))
        pl.when(jnp.logical_not(here_too))(lambda: drain(r3.at[pl.ds(0, split)], rsem.at[2 + b]))

    diagonal = iota((batch, WIDE), 0) == iota((batch, WIDE), 1)

    def send_4(b):
        got = r3[pl.ds(b * split, split)]
        turned = pltpu.roll(got, 4, 1)
        pairs = (split // 2, 2, 8, WIDE)
        top3 = iota((split // 2, 8, WIDE), 1) < 4
        got, turned = got.reshape(pairs), turned.reshape(pairs)
        tokens = [
            jnp.where(top3, got[:, 0], turned[:, 1]).reshape(batch, WIDE),
            jnp.where(top3, turned[:, 0], got[:, 1]).reshape(batch, WIDE),
        ]
        squares = jnp.sum(tokens[0] * tokens[0] + tokens[1] * tokens[1], axis=1, keepdims=True)
        scaled = [(tokens[f] * pack[f, 8:9, :]).astype(BF16) for f in range(2)]
        logits = jnp.sum(
            scaled[0].astype(F32) * pack[0, 9:10, :] + scaled[1].astype(F32) * pack[1, 9:10, :],
            axis=1,
            keepdims=True,
        )
        scaled = jnp.concatenate(scaled, axis=1)
        for n, stat in enumerate((squares, logits)):
            s7[b, n : n + 1] = jnp.sum(jnp.where(diagonal, stat, 0.0), axis=0, keepdims=True)
        r7[b, here] = s7[b]
        gate = jnp.dot(scaled, wg_v[...].reshape(2 * WIDE, -1), preferred_element_type=F32).astype(BF16)
        up = jnp.dot(scaled, wu_v[...].reshape(2 * WIDE, -1), preferred_element_type=F32).astype(BF16)
        for d in range(nk):
            s4[b, d, 0:batch] = gate[:, d * WIDE : (d + 1) * WIDE]
            s4[b, d, batch : 2 * batch] = up[:, d * WIDE : (d + 1) * WIDE]
        r4[b, here] = s4[b, k]
        for n, offset in enumerate(chips):
            d = chip_at(offset)
            sem = rsem.at[(10 if n < remotes else 8) + b]
            remote(s4.at[b, d], r4.at[b, n], ssem.at[3], sem, (2 * d + core, e)).start()
            if n + 1 == remotes or n + 1 == here:
                for m in range(0 if n < remotes else remotes, n + 1):
                    to = (2 * chip_at(chips[m]) + core, e)
                    remote(s7.at[b], r7.at[b, m], ssem.at[6], rsem.at[14 + b], to).start()

    def send_5(b):
        drain(r4.at[b, pl.ds(0, here - remotes)], rsem.at[8 + b])
        sums = jnp.sum(r4[b, remotes:].astype(F32), axis=0)
        if remotes:
            drain(r4.at[b, pl.ds(0, remotes)], rsem.at[10 + b])
            sums = sums + jnp.sum(r4[b, 0:remotes].astype(F32), axis=0)
        gate, up = sums[0:batch], sums[batch:]
        drain(r7.at[b, pl.ds(0, here)], rsem.at[14 + b])
        stats = jnp.sum(r7[b], axis=0)

        def column(n):
            return jnp.sum(jnp.where(diagonal, stats[n : n + 1], 0.0), axis=1, keepdims=True)

        inverse = lax.rsqrt(column(0) / (width * nc) + EPS)
        score = jax.nn.sigmoid(column(1) * inverse).astype(BF16).astype(F32)
        gate = gate * inverse
        act = gate / (1.0 + jnp.exp(-gate)) * (up * inverse) * score
        act = act.astype(BF16)
        s5[b] = act
        score_v[b] = jnp.broadcast_to(score, (batch, WIDE))
        r5[b, pl.ds(k, 1)] = act[None]
        for offset in chips:
            d = chip_at(offset)
            remote(s5.at[b], r5.at[b, k], ssem.at[4], rsem.at[12 + b], (2 * d + core, e)).start()

    def send_6(b):
        drain(r5.at[b, pl.ds(0, nk - 1)], rsem.at[12 + b])
        act = jnp.concatenate([r5[b, d] for d in range(nk)], axis=1)
        made = lax.dot_general(
            act, wd_v[...].reshape(2 * WIDE, -1), (((1,), (1,)), ((), ())), preferred_element_type=F32
        )
        shown = iota((batch, WIDE), 1) >= width
        for f in range(2):
            block = jnp.where(shown, score_v[b], made[:, f * WIDE : (f + 1) * WIDE])
            s6[f, pl.ds(b * split, split)] = block.reshape(split, 4, WIDE)

        def back(t, f):
            remote(s6.at[f, t], r6.at[e], ssem.at[5], rsem.at[5], (2 * k + f, half * core + t)).start()

        for i in range(1, split + 1):
            t = b * split + ((turn + i) & (split - 1))
            for f in range(2):
                if i == split:
                    pl.when(jnp.logical_not(owner & (core == f) & (mine_in == b)))(functools.partial(back, t, f))
                else:
                    back(t, f)

    first = jnp.where((core == 1) & ((e < split) | (e >= ne - split)), 1, 0)
    second = 1 - first
    wait_3(first)
    for n in (9, 10):
        loads[n].wait()
        swaps[n - 8].wait_recv()
    send_4(first)
    wait_3(second)
    send_4(second)
    send_5(first)
    send_5(second)
    loads[11].wait()
    swaps[3].wait_recv()
    send_6(first)
    send_6(second)

    @pl.when(owner)
    def _():
        r6[pl.ds(e, 1)] = s6[core, pl.ds(turn, 1)]
        drain(r6.at[pl.ds(0, ne - 1)], rsem.at[5])

    @pl.when(jnp.logical_not(owner))
    def _():
        drain(r6, rsem.at[5])
        pltpu.make_async_copy(st_v, st_v, pair_recv.at[4]).wait()

    mixed = jnp.sum(jnp.where(hit_v[...] > 0.0, r6[...], 0.0), axis=0)
    stream = st_v[...]
    stream = jnp.where(core == 1, pltpu.roll(stream, 4, 0), stream)[0:4]
    out_ref[...] = stream[:, 0:width] + ROUTE * mixed[:, 0:width] / mixed[:, width : width + 1]

    swap.wait_send()
    drain(m1.at[pl.ds(0, nk - 1)], ssem.at[0])
    drain(m7.at[pl.ds(0, nk - 1)], ssem.at[7])
    drain(s2.at[pl.ds(0, nk - 1)], ssem.at[1])
    for b in range(2):
        drain(s4.at[b, pl.ds(0, nk - 1)], ssem.at[3])
        drain(r7.at[b, pl.ds(0, nk - 1)], ssem.at[6])
        drain(r5.at[b, pl.ds(0, nk - 1)], ssem.at[4])
    drain(r6.at[pl.ds(0, ne - 1)], ssem.at[5])

    @pl.when(owner)
    def _():
        for _ in far:
            drain(hid_v, ssem.at[2])
        pltpu.make_async_copy(st_v, st_v, pair_send.at[4]).wait()

    @pl.when(jnp.logical_not(owner))
    def _():
        drain(s2.at[0], ssem.at[1])
        drain(r6.at[0], ssem.at[5])

    for one in swaps:
        one.wait_send()


def per_device(nc, ne, *args):
    (queries, cache, lengths, w_uv, w_out, residual, gain, router, w_gate, w_up, w_down, ids) = args
    nk, half = nc // 2, ne // 2
    width, ff = w_gate.shape[1], w_gate.shape[2]
    split = half // 2
    batch = 4 * split
    hbm = pl.BlockSpec(memory_space=pltpu.HBM)
    vmem = lambda *shape, dtype=F32: pltpu.VMEM(shape, dtype)
    half_type = functools.partial(vmem, dtype=BF16)
    like = lambda x: pltpu.VMEM(x.shape, x.dtype)
    gain = gain.reshape(1, width)
    w_down = jnp.swapaxes(w_down, 1, 2)
    scratch = [
        like(queries), like(cache), pltpu.SMEM(lengths.shape, I32), like(w_uv), like(w_out), like(residual),
        like(gain), like(router),
        half_type(2, WIDE, ff), half_type(2, WIDE, ff), half_type(2, WIDE, ff), like(ids),
        vmem(2, 16, WIDE), vmem(ne, 4, WIDE), vmem(8, WIDE), vmem(8, WIDE),
        half_type(nk, 16, LATENT // 2 + WIDE), half_type(nk, 16, LATENT // 2 + WIDE),
        vmem(nk, 8, LATENT), vmem(nk, 8, WIDE), vmem(nk, 8, WIDE),
        half_type(nk, 16, LATENT // 2), half_type(nk, 16, LATENT // 2),
        vmem(nk, 2, WIDE), vmem(nk, 2, WIDE),
        vmem(nk, 8, WIDE), vmem(nc, 8, WIDE),
        vmem(half, 8, WIDE),
        half_type(2, nk, 2 * batch, WIDE), half_type(2, nk, 2 * batch, WIDE),
        vmem(2, 2, WIDE), vmem(2, nk, 2, WIDE),
        half_type(2, batch, WIDE), half_type(2, nk, batch, WIDE), vmem(2, batch, WIDE),
        vmem(2, half, 4, WIDE), vmem(ne, 4, WIDE),
        pltpu.SemaphoreType.DMA((12,)),
        pltpu.SemaphoreType.DMA((6,)), pltpu.SemaphoreType.DMA((6,)),
        pltpu.SemaphoreType.DMA((8,)), pltpu.SemaphoreType.DMA((17,)), pltpu.SemaphoreType.REGULAR, pltpu.SemaphoreType.REGULAR,
    ]
    return pl.pallas_call(
        functools.partial(kernel, nc, ne),
        out_shape=pltpu.VMEM((4, width), F32),
        in_specs=[hbm] * 12,
        out_specs=pl.BlockSpec(memory_space=pltpu.VMEM),
        scratch_shapes=scratch,
        compiler_params=pltpu.CompilerParams(
            collective_id=0, has_side_effects=True, vmem_limit_bytes=60 * 1024 * 1024
        ),
    )(queries, cache, lengths, w_uv, w_out, residual, gain, router, w_gate, w_up, w_down, ids)


def solution(mesh):
    in_specs = (
        P("ep", None, None),
        P("ep", "ctx", None),
        P("ep"),
        P("ctx", None, None),
        P("ctx", None),
        P("ep", "ctx"),
        P("ctx"),
        P("ep", "ctx"),
        P("ep", "ctx", None),
        P("ep", "ctx", None),
        P("ep", None, "ctx"),
        P("ep", None),
    )
    return jax.shard_map(
        functools.partial(per_device, mesh.shape["ctx"], mesh.shape["ep"]),
        mesh=mesh, in_specs=in_specs, out_specs=P("ep", "ctx"), check_vma=False,
    )
```

```python
import functools

import jax
import jax.numpy as jnp
from jax import lax
from jax.experimental import pallas as pl
from jax.experimental.pallas import tpu as pltpu
from jax.sharding import PartitionSpec as P

SCALE = 192.0 ** (-0.5)
FLOOR = -1e30
EPS = 1e-06
ROUTE = 2.5
LATENT = 512
WIDE = 128
MESH = pl.DeviceIdType.MESH
BF16, F32, I32 = jnp.bfloat16, jnp.float32, jnp.int32


def iota(shape, dim):
    return lax.broadcasted_iota(I32, shape, dim)


def split_two(x):
    high = x.astype(BF16).astype(F32)
    return high, x - high


def kernel(
    nc,
    ne,
    q_h, cache_h, len_h, wuv_h, wout_h, res_h, gain_h, router_h, wg_h, wu_h, wd_h, ids_h,
    out_ref,
    q_v, cache_v, len_s, wuv_v, wout_v, res_v, gain_v, router_v, wg_v, wu_v, wd_v, ids_v,
    pack, hit_v, st_v, hid_v,
    s1, p1, own_v, own_peak, own_total, m1, r1, m7, r8, s2, r2, r3, s4, r4, s7, r7, s5, r5, score_v, s6, r6,
    load_sem, pair_send, pair_recv, ssem, rsem, hello, known,
):
    nk, half = nc // 2, ne // 2
    width = res_h.shape[1]
    span = cache_h.shape[1]
    rows = 8 * nc
    split = half // 2
    batch = 4 * split
    c, e = lax.axis_index("ctx"), lax.axis_index("ep")
    k, core = c >> 1, c & 1
    side = e // half
    turn = e & (half - 1)
    mine_in = turn // split
    owner = core == side
    partner = 2 * k + 1 - core

    def load(n, src, dst):
        return pltpu.make_async_copy(src, dst, load_sem.at[n])

    loads = [
        load(0, q_h, q_v),
        load(1, cache_h, cache_v),
        load(2, len_h, len_s),
        load(3, res_h, res_v),
        load(4, gain_h, gain_v),
        load(5, router_h, router_v),
        load(6, ids_h, ids_v),
        load(7, wuv_h, wuv_v),
        load(8, wout_h, wout_v),
        load(9, wg_h.at[0], wg_v.at[core, pl.ds(0, width)]),
        load(10, wu_h.at[0], wu_v.at[core, pl.ds(0, width)]),
        load(11, wd_h.at[0], wd_v.at[core, pl.ds(0, width)]),
    ]
    for one in loads[:3]:
        one.start()

    place = jnp.where((core == 1) & (e >= half), ne - 1 - (e - half), e)
    base = core * half
    source = (place >= base) & (place < base + half)

    def at_place(p):
        return (c, jnp.where((core == 1) & (p >= half), ne - 1 - (p - half), p))

    xs = 4 if nk % 4 == 0 else nk
    ys = nk // xs
    hops = lambda o: min(o[0], ys - o[0]) + min(o[1], xs - o[1])
    chips = [(dy, dx) for dy in range(ys) for dx in range(xs) if (dy, dx) != (0, 0)]
    chips.sort(key=lambda o: -hops(o))
    remotes = len([o for o in chips if hops(o) > 2])
    here = len(chips)

    peers = {o: ((k // xs + o[0]) & (ys - 1)) * xs + ((k + o[1]) & (xs - 1)) for o in chips}

    def chip_at(offset):
        return peers[offset]

    barrier = pltpu.get_barrier_semaphore()

    def greet(to):
        pl.semaphore_signal(barrier, inc=1, device_id=to, device_id_type=MESH)

    for offset in chips:
        greet((2 * chip_at(offset) + side, e))

    @pl.when(owner)
    def _():
        greet((partner, e))

    def greet_ep(p, _):
        z = at_place(p)[1]
        greet((2 * k + jnp.where((core == 0) & (place < split), 0, z // half), z))
        return 0

    first_up = jnp.where(core == 0, jnp.where(source, place + 1, ne), jnp.maximum(place + 1, half))
    lax.fori_loop(first_up, ne, greet_ep, 0)
    greeted = jnp.where(
        owner,
        2 * (nk - 1) + place + jnp.where(core == 1, half - split, 0),
        1 + jnp.where(core == 0, split, 0),
    )

    def answer(p, _):
        pl.semaphore_signal(hello, inc=1, device_id=at_place(p), device_id_type=MESH)
        return 0

    far = sorted(range(1, ne), key=lambda i: -min(i, ne - i))

    def remote(src, dst, send, recv, to):
        return pltpu.make_async_remote_copy(
            src_ref=src, dst_ref=dst, send_sem=send, recv_sem=recv, device_id=to, device_id_type=MESH
        )

    def drain(ref, sem):
        pltpu.make_async_copy(ref, ref, sem).wait()

    for one in loads[3:7]:
        one.start()

    def tell_partner():
        pl.semaphore_signal(known, inc=1, device_id=(partner, e), device_id_type=MESH)

    loads[0].wait()
    row = iota((rows, rows), 0)
    other = row >= 8 * nk
    want = (row & 3) * (2 * nc) + 4 * ((row >> 3) - jnp.where(other, nk, 0)) + ((row >> 2) & 1)
    want = want + 2 * jnp.where(other, 1 - core, core)
    order = jnp.where(iota((rows, rows), 1) == want, 1.0, 0.0).astype(BF16)
    q = q_v[...].reshape(rows, q_v.shape[2])
    q = jnp.dot(order, q, preferred_element_type=F32).astype(BF16)
    loads[1].wait()
    for one in loads[7:]:
        one.start()
    loads[2].wait()
    keys = cache_v[...].reshape(4 * span, cache_v.shape[2])
    scores = lax.dot_general(q, keys, (((1,), (1,)), ((), ())), preferred_element_type=F32) * SCALE
    col = iota((1, 4 * span), 1)
    col_row = jnp.zeros_like(col)
    limit = jnp.full_like(col, len_s[0])
    for r in range(1, 4):
        past = col >= r * span
        col_row = jnp.where(past, r, col_row)
        limit = jnp.where(past, len_s[r], limit)
    position = c * span + col - col_row * span
    col_row = jnp.where(position < limit, col_row, -1)
    valid = (iota((rows, 4 * span), 0) & 3) == col_row
    masked = jnp.where(valid, scores, FLOOR)
    peak = jnp.max(masked, axis=1, keepdims=True).astype(BF16).astype(F32)

    @pl.when(jnp.logical_not(owner))
    def _():
        pl.semaphore_wait(barrier, greeted)
        tell_partner()

        @pl.when(core == 0)
        def _():
            lax.fori_loop(0, split, answer, 0)

    weights = jnp.where(valid, jnp.exp(masked - peak), 0.0).astype(BF16)
    total = jnp.sum(weights.astype(F32), axis=1, keepdims=True)
    summed = jnp.dot(weights, keys[:, :LATENT], preferred_element_type=F32)
    summed = summed.reshape(2, nk, 8, LATENT)
    hl = LATENT // 2
    chunks = range(0, hl, WIDE)
    peaks = jnp.broadcast_to(peak, (rows, WIDE)).reshape(2, nk, 8, WIDE)
    totals = jnp.broadcast_to(total, (rows, WIDE)).reshape(2, nk, 8, WIDE)
    side_lane = iota((nk, 8, WIDE), 2) < 64

    def put(ref, top, amount, parts):
        high, rest = split_two(amount)
        for n, a in enumerate(chunks):
            ref[:, :, a : a + WIDE] = jnp.concatenate([parts[n], parts[n + len(chunks)]], axis=1).astype(BF16)
        ref[:, :, hl:] = jnp.concatenate([top, jnp.where(side_lane, high, rest)], axis=1).astype(BF16)

    columns = range(0, LATENT, WIDE)
    put(s1, peaks[1], totals[1], [summed[1, :, :, a : a + WIDE] for a in columns])
    own_v[...] = summed[0]
    own_peak[...] = peaks[0]
    own_total[...] = totals[0]

    swap = remote(s1, p1, pair_send.at[5], pair_recv.at[5], (partner, e))

    @pl.when(owner)
    def _():
        pl.semaphore_wait(known, 1)
        swap.start()
        pl.semaphore_wait(barrier, greeted)
        tell_partner()
        lax.fori_loop(base, place, answer, 0)

    pl.when(jnp.logical_not(owner))(swap.start)

    mine = pl.ds(0, width)
    swaps = [
        remote(pack.at[core], pack.at[core], pair_send.at[0], pair_recv.at[0], (partner, e)),
        remote(wg_h.at[0], wg_v.at[core, mine], pair_send.at[1], pair_recv.at[1], (partner, e)),
        remote(wu_h.at[0], wu_v.at[core, mine], pair_send.at[2], pair_recv.at[2], (partner, e)),
        remote(wd_h.at[0], wd_v.at[core, mine], pair_send.at[3], pair_recv.at[3], (partner, e)),
    ]
    swap.wait_recv()

    def stats_of(x):
        x = x.astype(F32)
        return x[:, 0:8], x[:, 8:16]

    peaks, totals = stats_of(p1[:, :, hl:])
    totals = totals + pltpu.roll(totals, 64, 2)
    top = jnp.maximum(peaks, own_peak[...])
    from_own, from_other = jnp.exp(own_peak[...] - top), jnp.exp(peaks - top)
    lefts, rights = [], []
    for a in chunks:
        block = p1[:, :, a : a + WIDE].astype(F32)
        lefts.append(from_own * own_v[:, :, a : a + WIDE] + from_other * block[:, 0:8])
        rights.append(from_own * own_v[:, :, hl + a : hl + a + WIDE] + from_other * block[:, 8:16])
    for n, a in enumerate(chunks):
        m1[:, :, a : a + WIDE] = jnp.concatenate([lefts[n], rights[n]], axis=1).astype(BF16)
    eight = iota((nk, 8, WIDE), 1) == iota((nk, 8, WIDE), 2)
    for n, stat in enumerate((top, from_own * own_total[...] + from_other * totals)):
        m7[:, n : n + 1] = jnp.sum(jnp.where(eight, stat, 0.0), axis=1, keepdims=True)
    r1[here] = m1[k]
    r8[here] = m7[k]

    @pl.when(jnp.logical_not(owner))
    def _():
        pl.semaphore_wait(known, 1)

    for group in (chips[:remotes], chips[remotes:]):
        begin = chips.index(group[0]) if group else 0
        for n, offset in enumerate(group, begin):
            d = chip_at(offset)
            remote(m1.at[d], r1.at[n], ssem.at[0], rsem.at[0], (2 * d + core, e)).start()
        for n, offset in enumerate(group, begin):
            d = chip_at(offset)
            remote(m7.at[d], r8.at[n], ssem.at[7], rsem.at[16], (2 * d + core, e)).start()
    @pl.when((core == 0) & jnp.logical_not(owner))
    def _():
        lax.fori_loop(split, half, answer, 0)

    for one in loads[3:7]:
        one.wait()
    pack[pl.ds(core, 1)] = jnp.zeros((1, 16, WIDE), F32)
    wide_res = res_v[...].astype(F32)
    pack[core, 0:8, 0:width] = jnp.concatenate([wide_res, wide_res], axis=0)
    pack[core, 8:9, 0:width] = gain_v[...]
    pack[core, 9:10, 0:width] = router_v[...].astype(F32)
    blank = jnp.zeros((2, WIDE - width, wg_v.shape[2]), BF16)
    wg_v[:, width:WIDE, :] = blank
    wu_v[:, width:WIDE, :] = blank
    wd_v[:, width:WIDE, :] = blank
    ids = ids_v[...]
    for x in range(ne):
        hit = jnp.max(jnp.where(ids == x, 1.0, 0.0), axis=1, keepdims=True)
        hit_v[x] = jnp.broadcast_to(hit, (4, WIDE))

    for one in swaps:
        one.start()

    drain(r1.at[pl.ds(0, here)], rsem.at[0])
    drain(r8.at[pl.ds(0, here)], rsem.at[16])
    peaks, totals = (
        jnp.sum(jnp.where(eight, r8[:, n : n + 1], 0.0), axis=2, keepdims=True) for n in range(2)
    )
    factor = jnp.exp(peaks - jnp.max(peaks, axis=0)[None])
    denom = jnp.sum(factor * totals, axis=0)
    factor = jnp.broadcast_to(factor, (nk, 8, WIDE))
    columns = []
    for first in (0, 8):
        for a in chunks:
            block = r1[:, :, a : a + WIDE].astype(F32)[:, first : first + 8]
            columns.append(jnp.sum(factor * block, axis=0))
    latent = (jnp.concatenate(columns, axis=1) / denom).astype(BF16)

    loads[7].wait()
    first = jnp.dot(latent, wuv_v[0], preferred_element_type=F32)
    second = jnp.dot(latent, wuv_v[1], preferred_element_type=F32)
    upper = iota((8, WIDE), 0) < 4
    lane = iota((8, WIDE), 1)
    values = jnp.concatenate(
        [
            jnp.where(upper, first, pltpu.roll(first, 4, 0)),
            jnp.where(upper, pltpu.roll(second, 4, 0), second),
        ],
        axis=1,
    ).astype(BF16)
    loads[8].wait()
    group = min(4, nk)
    for g in range(0, nk, group):
        begin, size = 2 * width * g, 2 * width * group
        part = jnp.dot(values, wout_v[:, begin : begin + size], preferred_element_type=F32)
        part = jnp.concatenate([part, jnp.zeros((8, WIDE), F32)], axis=1)
        for i in range(group):
            a = 2 * width * i
            s2[g + i] = jnp.where(upper, part[:, a : a + WIDE], part[:, a + width : a + width + WIDE])

    def send_2(n, d, sem):
        remote(s2.at[d], r2.at[2 * n + core], ssem.at[1], rsem.at[sem], (2 * d + side, e)).start()

    for n, offset in enumerate(chips):
        send_2(n, chip_at(offset), 7 if n < remotes else 1)

    @pl.when(owner)
    def _():
        r2[2 * here + core] = s2[k]

    @pl.when(jnp.logical_not(owner))
    def _():
        send_2(here, k, 1)

    swaps[0].wait_recv()

    @pl.when(owner)
    def _():
        drain(r2.at[pl.ds(0, 2 * (here - remotes) + 1)], rsem.at[1])
        stream = jnp.where(upper, pack[0, 0:8], pack[1, 0:8])
        stream = stream + jnp.sum(r2[2 * remotes :], axis=0)
        if remotes:
            drain(r2.at[pl.ds(0, 2 * remotes)], rsem.at[7])
            stream = stream + jnp.sum(r2[0 : 2 * remotes], axis=0)
        stream = jnp.where(lane < width, stream, 0.0)
        hidden = stream.astype(BF16).astype(F32)
        hid_v[...] = hidden
        st_v[...] = stream
        r3[pl.ds(turn, 1)] = hidden[None]


        @pl.when(place < ne - 1)
        def _():
            pl.semaphore_wait(hello, ne - 1 - place)

        arrived = rsem.at[2 + mine_in]
        for i in far:
            z = (e + i) & (ne - 1)
            remote(hid_v, r3.at[turn], ssem.at[2], arrived, (c, z)).start()
        remote(st_v, st_v, pair_send.at[4], pair_recv.at[4], (partner, e)).start()

    def wait_3(b):
        here_too = owner & (mine_in == b)
        pl.when(here_too)(lambda: drain(r3.at[pl.ds(0, split - 1)], rsem.at[2 + b]))
        pl.when(jnp.logical_not(here_too))(lambda: drain(r3.at[pl.ds(0, split)], rsem.at[2 + b]))

    diagonal = iota((batch, WIDE), 0) == iota((batch, WIDE), 1)

    def send_4(b):
        got = r3[pl.ds(b * split, split)]
        turned = pltpu.roll(got, 4, 1)
        pairs = (split // 2, 2, 8, WIDE)
        top3 = iota((split // 2, 8, WIDE), 1) < 4
        got, turned = got.reshape(pairs), turned.reshape(pairs)
        tokens = [
            jnp.where(top3, got[:, 0], turned[:, 1]).reshape(batch, WIDE),
            jnp.where(top3, turned[:, 0], got[:, 1]).reshape(batch, WIDE),
        ]
        squares = jnp.sum(tokens[0] * tokens[0] + tokens[1] * tokens[1], axis=1, keepdims=True)
        scaled = [(tokens[f] * pack[f, 8:9, :]).astype(BF16) for f in range(2)]
        logits = jnp.sum(
            scaled[0].astype(F32) * pack[0, 9:10, :] + scaled[1].astype(F32) * pack[1, 9:10, :],
            axis=1,
            keepdims=True,
        )
        scaled = jnp.concatenate(scaled, axis=1)
        for n, stat in enumerate((squares, logits)):
            s7[b, n : n + 1] = jnp.sum(jnp.where(diagonal, stat, 0.0), axis=0, keepdims=True)
        r7[b, here] = s7[b]
        gate = jnp.dot(scaled, wg_v[...].reshape(2 * WIDE, -1), preferred_element_type=F32).astype(BF16)
        up = jnp.dot(scaled, wu_v[...].reshape(2 * WIDE, -1), preferred_element_type=F32).astype(BF16)
        for d in range(nk):
            s4[b, d, 0:batch] = gate[:, d * WIDE : (d + 1) * WIDE]
            s4[b, d, batch : 2 * batch] = up[:, d * WIDE : (d + 1) * WIDE]
        r4[b, here] = s4[b, k]
        for n, offset in enumerate(chips):
            d = chip_at(offset)
            sem = rsem.at[(10 if n < remotes else 8) + b]
            remote(s4.at[b, d], r4.at[b, n], ssem.at[3], sem, (2 * d + core, e)).start()
            if n + 1 == remotes or n + 1 == here:
                for m in range(0 if n < remotes else remotes, n + 1):
                    to = (2 * chip_at(chips[m]) + core, e)
                    remote(s7.at[b], r7.at[b, m], ssem.at[6], rsem.at[14 + b], to).start()

    def send_5(b):
        drain(r4.at[b, pl.ds(0, here - remotes)], rsem.at[8 + b])
        sums = jnp.sum(r4[b, remotes:].astype(F32), axis=0)
        if remotes:
            drain(r4.at[b, pl.ds(0, remotes)], rsem.at[10 + b])
            sums = sums + jnp.sum(r4[b, 0:remotes].astype(F32), axis=0)
        gate, up = sums[0:batch], sums[batch:]
        drain(r7.at[b, pl.ds(0, here)], rsem.at[14 + b])
        stats = jnp.sum(r7[b], axis=0)

        def column(n):
            return jnp.sum(jnp.where(diagonal, stats[n : n + 1], 0.0), axis=1, keepdims=True)

        inverse = lax.rsqrt(column(0) / (width * nc) + EPS)
        score = jax.nn.sigmoid(column(1) * inverse).astype(BF16).astype(F32)
        gate = gate * inverse
        act = gate / (1.0 + jnp.exp(-gate)) * (up * inverse) * score
        act = act.astype(BF16)
        s5[b] = act
        score_v[b] = jnp.broadcast_to(score, (batch, WIDE))
        r5[b, pl.ds(k, 1)] = act[None]
        for offset in chips:
            d = chip_at(offset)
            remote(s5.at[b], r5.at[b, k], ssem.at[4], rsem.at[12 + b], (2 * d + core, e)).start()

    def send_6(b):
        drain(r5.at[b, pl.ds(0, nk - 1)], rsem.at[12 + b])
        act = jnp.concatenate([r5[b, d] for d in range(nk)], axis=1)
        made = lax.dot_general(
            act, wd_v[...].reshape(2 * WIDE, -1), (((1,), (1,)), ((), ())), preferred_element_type=F32
        )
        shown = iota((batch, WIDE), 1) >= width
        for f in range(2):
            block = jnp.where(shown, score_v[b], made[:, f * WIDE : (f + 1) * WIDE])
            s6[f, pl.ds(b * split, split)] = block.reshape(split, 4, WIDE)

        def back(t, f):
            remote(s6.at[f, t], r6.at[e], ssem.at[5], rsem.at[5], (2 * k + f, half * core + t)).start()

        for i in range(split):
            t = b * split + i
            back(t, partner - 2 * k)
            pl.when(jnp.logical_not(owner & (t == turn)))(functools.partial(back, t, core))

    first = jnp.where((core == 1) & ((e < split) | (e >= ne - split)), 1, 0)
    second = 1 - first
    wait_3(first)
    for n in (9, 10):
        loads[n].wait()
        swaps[n - 8].wait_recv()
    send_4(first)
    wait_3(second)
    send_4(second)
    send_5(first)
    send_5(second)
    loads[11].wait()
    swaps[3].wait_recv()
    send_6(first)
    send_6(second)

    @pl.when(owner)
    def _():
        r6[pl.ds(e, 1)] = s6[core, pl.ds(turn, 1)]
        drain(r6.at[pl.ds(0, ne - 1)], rsem.at[5])

    @pl.when(jnp.logical_not(owner))
    def _():
        drain(r6, rsem.at[5])
        pltpu.make_async_copy(st_v, st_v, pair_recv.at[4]).wait()

    mixed = jnp.sum(jnp.where(hit_v[...] > 0.0, r6[...], 0.0), axis=0)
    stream = st_v[...]
    stream = jnp.where(core == 1, pltpu.roll(stream, 4, 0), stream)[0:4]
    out_ref[...] = stream[:, 0:width] + ROUTE * mixed[:, 0:width] / mixed[:, width : width + 1]

    swap.wait_send()
    drain(m1.at[pl.ds(0, nk - 1)], ssem.at[0])
    drain(m7.at[pl.ds(0, nk - 1)], ssem.at[7])
    drain(s2.at[pl.ds(0, nk - 1)], ssem.at[1])
    for b in range(2):
        drain(s4.at[b, pl.ds(0, nk - 1)], ssem.at[3])
        drain(r7.at[b, pl.ds(0, nk - 1)], ssem.at[6])
        drain(r5.at[b, pl.ds(0, nk - 1)], ssem.at[4])
    drain(r6.at[pl.ds(0, ne - 1)], ssem.at[5])

    @pl.when(owner)
    def _():
        for _ in far:
            drain(hid_v, ssem.at[2])
        pltpu.make_async_copy(st_v, st_v, pair_send.at[4]).wait()

    @pl.when(jnp.logical_not(owner))
    def _():
        drain(s2.at[0], ssem.at[1])
        drain(r6.at[0], ssem.at[5])

    for one in swaps:
        one.wait_send()


def per_device(nc, ne, *args):
    (queries, cache, lengths, w_uv, w_out, residual, gain, router, w_gate, w_up, w_down, ids) = args
    nk, half = nc // 2, ne // 2
    width, ff = w_gate.shape[1], w_gate.shape[2]
    split = half // 2
    batch = 4 * split
    hbm = pl.BlockSpec(memory_space=pltpu.HBM)
    vmem = lambda *shape, dtype=F32: pltpu.VMEM(shape, dtype)
    half_type = functools.partial(vmem, dtype=BF16)
    like = lambda x: pltpu.VMEM(x.shape, x.dtype)
    gain = gain.reshape(1, width)
    w_down = jnp.swapaxes(w_down, 1, 2)
    scratch = [
        like(queries), like(cache), pltpu.SMEM(lengths.shape, I32), like(w_uv), like(w_out), like(residual),
        like(gain), like(router),
        half_type(2, WIDE, ff), half_type(2, WIDE, ff), half_type(2, WIDE, ff), like(ids),
        vmem(2, 16, WIDE), vmem(ne, 4, WIDE), vmem(8, WIDE), vmem(8, WIDE),
        half_type(nk, 16, LATENT // 2 + WIDE), half_type(nk, 16, LATENT // 2 + WIDE),
        vmem(nk, 8, LATENT), vmem(nk, 8, WIDE), vmem(nk, 8, WIDE),
        half_type(nk, 16, LATENT // 2), half_type(nk, 16, LATENT // 2),
        vmem(nk, 2, WIDE), vmem(nk, 2, WIDE),
        vmem(nk, 8, WIDE), vmem(nc, 8, WIDE),
        vmem(half, 8, WIDE),
        half_type(2, nk, 2 * batch, WIDE), half_type(2, nk, 2 * batch, WIDE),
        vmem(2, 2, WIDE), vmem(2, nk, 2, WIDE),
        half_type(2, batch, WIDE), half_type(2, nk, batch, WIDE), vmem(2, batch, WIDE),
        vmem(2, half, 4, WIDE), vmem(ne, 4, WIDE),
        pltpu.SemaphoreType.DMA((12,)),
        pltpu.SemaphoreType.DMA((6,)), pltpu.SemaphoreType.DMA((6,)),
        pltpu.SemaphoreType.DMA((8,)), pltpu.SemaphoreType.DMA((17,)), pltpu.SemaphoreType.REGULAR, pltpu.SemaphoreType.REGULAR,
    ]
    return pl.pallas_call(
        functools.partial(kernel, nc, ne),
        out_shape=pltpu.VMEM((4, width), F32),
        in_specs=[hbm] * 12,
        out_specs=pl.BlockSpec(memory_space=pltpu.VMEM),
        scratch_shapes=scratch,
        compiler_params=pltpu.CompilerParams(
            collective_id=0, has_side_effects=True, vmem_limit_bytes=60 * 1024 * 1024
        ),
    )(queries, cache, lengths, w_uv, w_out, residual, gain, router, w_gate, w_up, w_down, ids)


def solution(mesh):
    in_specs = (
        P("ep", None, None),
        P("ep", "ctx", None),
        P("ep"),
        P("ctx", None, None),
        P("ctx", None),
        P("ep", "ctx"),
        P("ctx"),
        P("ep", "ctx"),
        P("ep", "ctx", None),
        P("ep", "ctx", None),
        P("ep", None, "ctx"),
        P("ep", None),
    )
    return jax.shard_map(
        functools.partial(per_device, mesh.shape["ctx"], mesh.shape["ep"]),
        mesh=mesh, in_specs=in_specs, out_specs=P("ep", "ctx"), check_vma=False,
    )
```
